32 devices in a mesh: ctx: 16 (over z, y, core), tp: 2 (over x).
Axes of the slice: x: 2, y: 2, z: 4, core: 2. Of those that a mesh axis runs over, the one named last changes fastest.
Arguments:
- query_in: bfloat16 [256, 4096], P('tp', 'ctx'), may hold values from -6 to 6
- key_in: bfloat16 [256, 4096], P('tp', 'ctx'), may hold values from -6 to 6
- value_in: bfloat16 [256, 4096], P('tp', 'ctx'), may hold values from -6 to 6
- short_kernel: float32 [3, 256, 7], P(None, 'tp'), may hold values from -2 to 2
- basis_weight: float32 [64, 33], replicated, may hold values from -96 to 96
- basis_bias: float32 [64], replicated, may hold values from -3.140625 to 3.140625
- filter_proj: float32 [256, 64], P('tp'), may hold values from -0.75 to 0.75
- decay_rate: float32 [256], P('tp'), as said below
- skip_gain: float32 [256], P('tp'), may hold values from -3 to 3
- grad_out: bfloat16 [256, 4096], P('tp', 'ctx'), may hold values from -6 to 6
Outputs:
- mixed: bfloat16 [256, 4096], P('tp', 'ctx')
- grad_query: bfloat16 [256, 4096], P('tp', 'ctx')
- grad_key: bfloat16 [256, 4096], P('tp', 'ctx')
- grad_value: bfloat16 [256, 4096], P('tp', 'ctx')
- grad_proj: float32 [256, 64], P('tp')
- grad_basis: float32 [64, 33], replicated
The draws below stay inside these ranges and needn't reach their ends.
Inputs may be any that keep to these rules, and one draw needn't show every extreme that they name: decay_rate is positive in every channel.
All inputs are finite; a program needn't handle non-finite values.
Results may differ from the reference program's by a relative error of at most 0.0066.
Values may be sent and summed in bfloat16 or wider, within the bound.
A program may use at most 64 MiB of HBM per device.

```python
import math
import jax
import jax.numpy as jnp
from jax import lax

CH_DEV = 128
FEAT = 64
NFREQ = 16
KSHORT = 7
EMB = 33
TOKENS = 4096
CHANNELS = 256
N_TP = 2


def draw_decay_rate(key, part):
    pick_key, slow_key, fast_key = jax.random.split(key, 3)
    slow_share = 0.5
    slow_rate = jax.random.uniform(slow_key, (CHANNELS,), jnp.float32, 0.2, 2.0)
    fast_len = jax.random.uniform(fast_key, (CHANNELS,), jnp.float32, 30.0, 50.0)
    fast_rate = TOKENS / fast_len
    chosen = jax.random.bernoulli(pick_key, slow_share, (CHANNELS,))
    return jnp.where(chosen, slow_rate, fast_rate).astype(jnp.float32)


def steps_of(rng, extent, shards, low, largest):
    loudness = 1.0
    for dim, parts in shards:
        draws = jax.random.uniform(jax.random.fold_in(jax.random.fold_in(rng, 6), dim), (parts,), jnp.float32, low / len(shards), largest / len(shards))
        loudness = loudness * jnp.repeat(jnp.exp(draws), extent[dim] // parts).reshape((-1,) + (1,) * (len(extent) - 1 - dim))
    return loudness


def noise(rng, shape, deviation, most, cuts=(), kind=jnp.bfloat16):
    array = jax.random.normal(rng, shape, jnp.float32) * deviation
    if len(cuts) > 0:
        array = steps_of(rng, shape, cuts, -0.22, 0.18) * array
    return jnp.clip(array, min=-most, max=most).astype(kind)


def setup_inputs(seed: int = 0) -> dict:
    keys = jax.random.split(jax.random.key(seed), 11)
    query_in = noise(keys[0], (CHANNELS, TOKENS), 1.0, 6.0, ((0, 2), (1, 16)))
    key_in = noise(keys[1], (CHANNELS, TOKENS), 1.0, 6.0, ((0, 2), (1, 16)))
    value_in = noise(keys[2], (CHANNELS, TOKENS), 1.0, 6.0, ((0, 2), (1, 16)))
    short_kernel = noise(keys[3], (3, CHANNELS, KSHORT), KSHORT ** -0.5, 2.0, ((1, 2),), jnp.float32)
    basis_weight = jnp.clip(jax.random.uniform(keys[4], (FEAT, EMB), jnp.float32, -96.0, 96.0), -96.0, 96.0)
    basis_bias = jnp.clip(jax.random.uniform(keys[5], (FEAT,), jnp.float32, -3.140625, 3.140625), -3.140625, 3.140625)
    filter_proj = noise(keys[6], (CHANNELS, FEAT), FEAT ** -0.5, 0.75, ((0, 2),), jnp.float32)
    decay_rate = draw_decay_rate(jax.random.fold_in(keys[10], 71), 0)
    skip_gain = noise(keys[8], (CHANNELS,), 1.0, 3.0, ((0, 2),), jnp.float32)
    grad_out = noise(keys[9], (CHANNELS, TOKENS), 1.0, 6.0, ((0, 2), (1, 16)))
    return {"query_in": query_in, "key_in": key_in, "value_in": value_in, "short_kernel": short_kernel, "basis_weight": basis_weight, "basis_bias": basis_bias, "filter_proj": filter_proj, "decay_rate": decay_rate, "skip_gain": skip_gain, "grad_out": grad_out}


PRECISE = lax.Precision.HIGHEST

def features(offset_pos, num_pos, seq_total, num_freq):
    positions = offset_pos + jnp.arange(num_pos, dtype=jnp.int32)
    pieces = [positions.astype(jnp.float32) / seq_total]
    for harmonic in range(1, num_freq + 1):
        angles = (harmonic * positions % seq_total).astype(jnp.float32) * (2.0 * math.pi / seq_total)
        pieces.append(jnp.cos(angles))
        pieces.append(jnp.sin(angles))
    return jnp.stack(pieces)

def window(decay_rate, offset_pos, num_pos, seq_total):
    positions = (offset_pos + jnp.arange(num_pos, dtype=jnp.int32)).astype(jnp.float32)
    energy = jnp.expm1(-2.0 * decay_rate) / jnp.expm1(-2.0 * decay_rate / seq_total)
    return jnp.exp(-(decay_rate[:, None] * positions[None, :]) / seq_total) / jnp.sqrt(energy)[:, None]

def featurize(signal, kernel):
    num_taps = kernel.shape[1]
    result = kernel[:, 0:1] * signal
    for offset in range(1, num_taps):
        shifted = jnp.pad(signal[:, :-offset], ((0, 0), (offset, 0)))
        result = result + kernel[:, offset:offset + 1] * shifted
    return result

def featurize_back(signal, kernel):
    num_taps = kernel.shape[1]
    result = kernel[:, 0:1] * signal
    for offset in range(1, num_taps):
        shifted = jnp.pad(signal[:, offset:], ((0, 0), (0, offset)))
        result = result + kernel[:, offset:offset + 1] * shifted
    return result

def long_block(operands):
    filter_block, carried_block, grad_block, skip_block = operands
    seq_total = filter_block.shape[1]
    padded_len = 2 * seq_total
    carried_wide = carried_block.astype(jnp.float32)
    grad_wide = grad_block.astype(jnp.float32)
    carried_spec = jnp.fft.rfft(carried_wide, n=padded_len)
    filter_spec = jnp.fft.rfft(filter_block.astype(jnp.float32), n=padded_len)
    grad_spec = jnp.fft.rfft(grad_wide, n=padded_len)
    long_part = jnp.fft.irfft(filter_spec * carried_spec, n=padded_len)[:, :seq_total] + skip_block[:, None] * carried_wide
    carried_grad = jnp.fft.irfft(jnp.conj(filter_spec) * grad_spec, n=padded_len)[:, :seq_total] + skip_block[:, None] * grad_wide
    filter_grad = jnp.fft.irfft(jnp.conj(carried_spec) * grad_spec, n=padded_len)[:, :seq_total]
    return (long_part.astype(jnp.bfloat16), carried_grad.astype(jnp.bfloat16), filter_grad.astype(jnp.bfloat16))

def reference(query_in, key_in, value_in, short_kernel, basis_weight, basis_bias, filter_proj, decay_rate, skip_gain, grad_out):
    query_feat = featurize(query_in.astype(jnp.float32), short_kernel[0])
    key_feat = featurize(key_in.astype(jnp.float32), short_kernel[1])
    value_feat = featurize(value_in.astype(jnp.float32), short_kernel[2])
    carried = (key_feat * value_feat).astype(jnp.bfloat16)
    basis_rows = features(0, TOKENS, TOKENS, NFREQ)
    hidden_in = jnp.dot(basis_weight, basis_rows, precision=PRECISE, preferred_element_type=jnp.float32) + basis_bias[:, None]
    activation = jnp.sin(hidden_in)
    envelope = window(decay_rate, 0, TOKENS, TOKENS)
    filter_full = (jnp.dot(filter_proj, activation, precision=PRECISE, preferred_element_type=jnp.float32) * envelope).astype(jnp.bfloat16)
    grad_wide = grad_out.astype(jnp.float32)
    grad_long = (grad_wide * query_feat).astype(jnp.bfloat16)
    grouped = (filter_full.reshape(N_TP, CH_DEV, TOKENS), carried.reshape(N_TP, CH_DEV, TOKENS), grad_long.reshape(N_TP, CH_DEV, TOKENS), skip_gain.reshape(N_TP, CH_DEV))
    long_out, carried_grad, filter_grad = lax.map(long_block, grouped)
    long_out = long_out.reshape(CHANNELS, TOKENS)
    carried_grad = carried_grad.reshape(CHANNELS, TOKENS)
    filter_grad = filter_grad.reshape(CHANNELS, TOKENS)
    long_wide = long_out.astype(jnp.float32)
    mixed = (query_feat * long_wide).astype(jnp.bfloat16)
    grad_query_feat = (grad_wide * long_wide).astype(jnp.bfloat16)
    carried_wide = carried_grad.astype(jnp.float32)
    grad_key_feat = (carried_wide * value_feat).astype(jnp.bfloat16)
    grad_value_feat = (carried_wide * key_feat).astype(jnp.bfloat16)
    grad_query = featurize_back(grad_query_feat.astype(jnp.float32), short_kernel[0]).astype(jnp.bfloat16)
    grad_key = featurize_back(grad_key_feat.astype(jnp.float32), short_kernel[1]).astype(jnp.bfloat16)
    grad_value = featurize_back(grad_value_feat.astype(jnp.float32), short_kernel[2]).astype(jnp.bfloat16)
    grad_raw = filter_grad.astype(jnp.float32) * envelope
    grad_proj = jnp.dot(grad_raw, activation.T, precision=PRECISE, preferred_element_type=jnp.float32) * (1.0 / math.sqrt(TOKENS))
    grad_hidden = jnp.dot(filter_proj.T, grad_raw, precision=PRECISE, preferred_element_type=jnp.float32) * jnp.cos(hidden_in)
    grad_basis = jnp.dot(grad_hidden, basis_rows.T, precision=PRECISE, preferred_element_type=jnp.float32) * math.sqrt(FEAT / (TOKENS * CHANNELS))
    return (mixed, grad_query, grad_key, grad_value, grad_proj, grad_basis)
```

```python
import functools
import math

import jax
import jax.numpy as jnp
import ml_dtypes
import numpy as np
from jax import lax
from jax.experimental import pallas as pl
from jax.experimental.pallas import tpu as pltpu
from jax.sharding import PartitionSpec as P

MESH = pl.DeviceIdType.MESH
BF16 = jnp.bfloat16
F32 = jnp.float32
LANES = 128
BAND = 40


def halves(table):
    high = table.astype(ml_dtypes.bfloat16)
    low = (table - high.astype(np.float64)).astype(ml_dtypes.bfloat16)
    return high, low


def constant_tables(seq_total, chans, num_freq):
    blocks = seq_total // LANES
    kept = blocks + 1
    period = 2 * blocks
    spec_rows = -(-kept * chans // 8) * 8
    eye = np.eye(chans)
    k1 = np.arange(kept)
    n1 = np.arange(blocks)
    n2 = np.arange(LANES)
    turn = 2.0 * np.pi * ((k1[:, None] * n1[None, :]) % period) / period
    fwd = np.zeros((2, spec_rows, blocks * chans))
    fwd[0, : kept * chans] = np.kron(np.cos(turn), eye)
    fwd[1, : kept * chans] = np.kron(-np.sin(turn), eye)
    weight = np.where((k1 == 0) | (k1 == blocks), 1.0, 2.0)[:, None] / (2.0 * seq_total)
    back = np.zeros((2, spec_rows, blocks * chans))
    back[0, : kept * chans] = np.kron(weight * np.cos(turn), eye)
    back[1, : kept * chans] = np.kron(-weight * np.sin(turn), eye)
    back = back.reshape(2 * spec_rows, blocks * chans).T.copy()
    fwd = fwd.reshape(2 * spec_rows, blocks * chans)
    twist = 2.0 * np.pi * ((k1[:, None] * n2[None, :]) % (2 * seq_total)) / (2 * seq_total)
    twiddle = np.zeros((2, spec_rows, LANES))
    twiddle[0, : kept * chans] = np.repeat(np.cos(twist), chans, axis=0)
    twiddle[1, : kept * chans] = np.repeat(-np.sin(twist), chans, axis=0)
    small = 2.0 * np.pi * ((n2[:, None] * n2[None, :]) % LANES) / LANES
    cos, sin = np.cos(small), np.sin(small)
    inner = np.block([[cos, -sin], [sin, cos]])
    inner_back = np.block([[cos, sin], [-sin, cos]])
    positions = np.arange(seq_total)
    basis = np.zeros((BAND, seq_total))
    basis[0] = positions / seq_total
    for harmonic in range(1, num_freq + 1):
        angles = 2.0 * np.pi * ((harmonic * positions) % seq_total) / seq_total
        basis[2 * harmonic - 1] = np.cos(angles)
        basis[2 * harmonic] = np.sin(angles)
    basis[2 * num_freq + 1] = 1.0
    first = basis.astype(ml_dtypes.bfloat16)
    rest = basis - first.astype(np.float64)
    second = rest.astype(ml_dtypes.bfloat16)
    third = (rest - second.astype(np.float64)).astype(ml_dtypes.bfloat16)
    rim = np.zeros((16, seq_total), ml_dtypes.bfloat16)
    basis_table = np.concatenate([first, second, third, first, second, first, rim])
    return (
        basis_table,
        *halves(fwd),
        *halves(back),
        *halves(inner),
        *halves(inner_back),
        twiddle.astype(np.float32),
    )


def dot(left, right):
    return jnp.dot(left, right, preferred_element_type=F32)


def dot_lanes(left, right):
    return lax.dot_general(left, right, (((1,), (1,)), ((), ())), preferred_element_type=F32)


def split(value):
    high = value.astype(BF16)
    return high, (value - high.astype(F32)).astype(BF16)


def sine_cosine(angle):
    quarter = jnp.floor(angle * (2.0 / math.pi) + 0.5)
    rest = angle - quarter * 1.5703125
    rest = rest - quarter * 4.837512969970703125e-4
    rest = rest - quarter * 7.54978995489188216e-8
    square = rest * rest
    sine = rest + rest * square * (
        -1.6666654611e-1 + square * (8.3321608736e-3 + square * -1.9515295891e-4)
    )
    cosine = (
        1.0
        - 0.5 * square
        + square
        * square
        * (4.166664568298827e-2 + square * (-1.388731625493765e-3 + square * 2.443315711809948e-5))
    )
    turns = quarter.astype(jnp.int32)
    odd = (turns & 1) == 1
    sin_out = jnp.where(odd, cosine, sine)
    cos_out = jnp.where(odd, sine, cosine)
    sin_out = jnp.where((turns & 2) == 2, -sin_out, sin_out)
    cos_out = jnp.where(((turns + 1) & 2) == 2, -cos_out, cos_out)
    return sin_out, cos_out


def mixer_kernel(
    dims,
    kv_ref,
    qg_ref,
    params_ref,
    weight_ref,
    basis_ref,
    fwd_hi,
    fwd_lo,
    back_hi,
    back_lo,
    inner_hi,
    inner_lo,
    inv_hi,
    inv_lo,
    twiddle_ref,
    mq_out,
    kv_out,
    proj_out,
    basis_out,
    kv_in,
    qg_in,
    mq_send,
    kv_send,
    mq_back,
    kv_back,
    act_buf,
    cos_buf,
    filt_buf,
    rows_buf,
    part_buf,
    part_in,
    sum_buf,
    sum_in,
    gp_buf,
    gp_in,
    send_sems,
    recv_sems,
):
    ctx_size, tp_size, chans, seq_total, taps, feat, emb, tp_chans = dims
    me = lax.axis_index("ctx")
    my_tp = lax.axis_index("tp")
    blocks = seq_total // LANES
    rows = blocks * chans
    spec_rows = twiddle_ref.shape[1]
    slab = 2 * chans
    all_size = ctx_size * tp_size
    my_id = my_tp * ctx_size + me
    chunk = 512

    def others(body):
        def step(offset, carry):
            body(lax.rem(me + offset, ctx_size))
            return carry

        lax.fori_loop(1, ctx_size, step, 0)

    def all_others(body):
        def step(offset, carry):
            other = lax.rem(my_id + offset, all_size)
            body(lax.rem(other, ctx_size), other // ctx_size)
            return carry

        lax.fori_loop(1, all_size, step, 0)

    barrier = pltpu.get_barrier_semaphore()

    def greet(ctx, tp):
        pl.semaphore_signal(
            barrier, inc=1, device_id={"ctx": ctx, "tp": tp}, device_id_type=MESH
        )

    all_others(greet)
    pl.semaphore_wait(barrier, all_size - 1)

    def push(src, dst, lane, ctx, tp):
        pltpu.make_async_remote_copy(
            src_ref=src,
            dst_ref=dst,
            send_sem=send_sems.at[lane],
            recv_sem=recv_sems.at[lane],
            device_id={"ctx": ctx, "tp": tp},
            device_id_type=MESH,
        ).start()

    def settle(ref, sem, count):
        part = ref.at[pl.ds(0, count)]
        pltpu.make_async_copy(part, part, sem).wait()

    others(lambda peer: push(kv_ref.at[peer], kv_in.at[me], 0, peer, my_tp))
    others(lambda peer: push(qg_ref.at[peer], qg_in.at[me], 1, peer, my_tp))
    kv_in[me] = kv_ref[me]
    qg_in[me] = qg_ref[me]

    params = params_ref[me]

    def column(index):
        wide = jnp.broadcast_to(params[:, index : index + 1], (8, LANES))
        return jnp.concatenate([wide] * (rows // 8), axis=0)

    tap_at = feat
    decay = column(feat + 3 * taps)
    inv_energy = column(feat + 3 * taps + 1)
    skip = column(feat + 3 * taps + 2)

    lane_ids = lax.broadcasted_iota(jnp.int32, (rows, LANES), 1)
    row_ids = lax.broadcasted_iota(jnp.int32, (rows, LANES), 0)
    positions = ((row_ids // chans) * LANES + lane_ids).astype(F32)
    envelope = jnp.exp(-(decay * positions) / seq_total) * inv_energy

    weight = weight_ref[...]
    w_one = weight.astype(BF16)
    w_rest = weight - w_one.astype(F32)
    w_two = w_rest.astype(BF16)
    w_three = (w_rest - w_two.astype(F32)).astype(BF16)
    place = lax.broadcasted_iota(jnp.int32, weight.shape, 1)
    w_stack = jnp.where(
        place < 3 * BAND,
        w_one.astype(F32),
        jnp.where(place < 5 * BAND, w_two.astype(F32), w_three.astype(F32)),
    ).astype(BF16)

    own_proj = params[:, :feat]
    proj_hi, proj_lo = split(own_proj)
    proj_hi = proj_hi.astype(F32)
    proj_lo = proj_lo.astype(F32)
    proj_stack = jnp.concatenate(
        [
            jnp.concatenate([proj_hi, proj_hi], axis=1),
            jnp.concatenate([proj_lo, proj_lo], axis=1),
        ],
        axis=0,
    ).astype(BF16)

    def filter_step(index, carry):
        start = pl.multiple_of(index * chunk, chunk)
        here = pl.ds(start, chunk)
        hidden = dot(w_stack, basis_ref[:, here])
        act, cosine = sine_cosine(hidden)
        cos_buf[:, here] = cosine
        act_hi, act_lo = split(act)
        act_buf[0:feat, here] = act_hi
        act_buf[feat : 2 * feat, here] = act_lo
        both = dot(proj_stack, act_buf[:, here])
        piece = both[0:8] + both[8:16]
        for block in range(chunk // LANES):
            at = pl.multiple_of((index * (chunk // LANES) + block) * chans, chans)
            filt_buf[pl.ds(at, chans), :] = piece[
                0:chans, block * LANES : (block + 1) * LANES
            ]
        return carry

    lax.fori_loop(0, seq_total // chunk, filter_step, 0)
    filt = (filt_buf[...] * envelope).astype(BF16)

    def spectrum(signal):
        outer = dot(fwd_hi[...], signal) + dot(fwd_lo[...], signal)
        out_re, out_im = outer[:spec_rows], outer[spec_rows:]
        tw_re, tw_im = twiddle_ref[0], twiddle_ref[1]
        turned = jnp.concatenate(
            [out_re * tw_re - out_im * tw_im, out_re * tw_im + out_im * tw_re], axis=1
        )
        high, low = split(turned)
        spec = dot(high, inner_hi[...]) + dot(high, inner_lo[...]) + dot(low, inner_hi[...])
        return spec[:, :LANES], spec[:, LANES:]

    def restore(spec_re, spec_im):
        high, low = split(jnp.concatenate([spec_re, spec_im], axis=1))
        section = dot(high, inv_hi[...]) + dot(high, inv_lo[...]) + dot(low, inv_hi[...])
        sec_re, sec_im = section[:, :LANES], section[:, LANES:]
        tw_re, tw_im = twiddle_ref[0], twiddle_ref[1]
        turned = jnp.concatenate(
            [sec_re * tw_re + sec_im * tw_im, sec_im * tw_re - sec_re * tw_im], axis=0
        )
        high, low = split(turned)
        return dot(back_hi[...], high) + dot(back_lo[...], high) + dot(back_hi[...], low)

    def to_rows(ref, index):
        if slab % 16 == 0:
            return ref[:, index].reshape(rows, LANES).astype(F32)
        for source in range(ctx_size):
            rows_buf[source * slab : (source + 1) * slab, :] = ref[source, index].astype(F32)
        return rows_buf[...]

    def from_rows(ref, index, value):
        if slab % 16 == 0:
            ref[:, index] = value.reshape(ctx_size, slab, LANES)
        else:
            rows_buf[...] = value.astype(F32)
            for target in range(ctx_size):
                ref[target, index] = rows_buf[target * slab : (target + 1) * slab, :].astype(BF16)

    blank = jnp.zeros((chans, LANES), F32)

    def down(value):
        if chans % 8 == 0:
            return jnp.concatenate([blank, value[: rows - chans]], axis=0)
        return jnp.where(row_ids < chans, 0.0, pltpu.roll(value, chans, 0))

    def up(value):
        if chans % 8 == 0:
            return jnp.concatenate([value[chans:], blank], axis=0)
        return jnp.where(row_ids >= rows - chans, 0.0, pltpu.roll(value, rows - chans, 0))

    def featurize(signal, which):
        result = column(tap_at + which * taps) * signal
        for offset in range(1, taps):
            turned = pltpu.roll(signal, offset, 1)
            shifted = jnp.where(lane_ids < offset, down(turned), turned)
            result = result + column(tap_at + which * taps + offset) * shifted
        return result

    def featurize_back(signal, which):
        result = column(tap_at + which * taps) * signal
        for offset in range(1, taps):
            turned = pltpu.roll(signal, LANES - offset, 1)
            shifted = jnp.where(lane_ids >= LANES - offset, up(turned), turned)
            result = result + column(tap_at + which * taps + offset) * shifted
        return result

    filt_re, filt_im = spectrum(filt)

    settle(kv_in, recv_sems.at[0], ctx_size - 1)
    key_feat = featurize(to_rows(kv_in, 0), 1)
    value_feat = featurize(to_rows(kv_in, 1), 2)
    carried = (key_feat * value_feat).astype(BF16)
    carried_re, carried_im = spectrum(carried)

    long_out = restore(
        filt_re * carried_re - filt_im * carried_im, filt_re * carried_im + filt_im * carried_re
    )
    long_out = (long_out + skip * carried.astype(F32)).astype(BF16).astype(F32)

    settle(qg_in, recv_sems.at[1], ctx_size - 1)
    query_feat = featurize(to_rows(qg_in, 0), 0)
    grad_wide = to_rows(qg_in, 1)
    from_rows(mq_send, 0, (query_feat * long_out).astype(BF16))
    grad_query_feat = (grad_wide * long_out).astype(BF16).astype(F32)
    from_rows(mq_send, 1, featurize_back(grad_query_feat, 0).astype(BF16))
    others(lambda peer: push(mq_send.at[peer], mq_back.at[me], 2, peer, my_tp))

    grad_long = (grad_wide * query_feat).astype(BF16)
    grad_re, grad_im = spectrum(grad_long)

    carried_grad = restore(
        filt_re * grad_re + filt_im * grad_im, filt_re * grad_im - filt_im * grad_re
    )
    carried_grad = (carried_grad + skip * grad_long.astype(F32)).astype(BF16).astype(F32)
    grad_key_feat = (carried_grad * value_feat).astype(BF16).astype(F32)
    grad_value_feat = (carried_grad * key_feat).astype(BF16).astype(F32)
    from_rows(kv_send, 0, featurize_back(grad_key_feat, 1).astype(BF16))
    from_rows(kv_send, 1, featurize_back(grad_value_feat, 2).astype(BF16))
    others(lambda peer: push(kv_send.at[peer], kv_back.at[me], 3, peer, my_tp))

    filter_grad = restore(
        carried_re * grad_re + carried_im * grad_im, carried_re * grad_im - carried_im * grad_re
    )
    grad_raw = filter_grad.astype(BF16).astype(F32) * envelope
    if chans % 8 == 0:
        raw_wide = jnp.concatenate(
            [grad_raw[block * chans : (block + 1) * chans] for block in range(blocks)], axis=1
        )
    else:
        rows_buf[...] = grad_raw
        raw_wide = jnp.concatenate(
            [
                jnp.concatenate(
                    [
                        rows_buf[block * chans : (block + 1) * chans, :],
                        jnp.zeros((8 - chans, LANES), F32),
                    ],
                    axis=0,
                )
                for block in range(blocks)
            ],
            axis=1,
        )
    raw_hi, raw_lo = split(raw_wide)
    raw_hi = raw_hi.astype(F32)
    raw_lo = raw_lo.astype(F32)
    raw_two = jnp.concatenate([raw_hi, raw_lo], axis=0).astype(BF16)
    gp_all = dot_lanes(raw_two, act_buf[...])
    gp_all = gp_all[0:8] + gp_all[8:16]
    gp = gp_all[:, :feat] + gp_all[:, feat : 2 * feat]
    gp_buf[...] = gp[0:chans] * (1.0 / math.sqrt(seq_total))
    others(lambda peer: push(gp_buf, gp_in.at[me], 4, peer, my_tp))

    turned_params = jnp.transpose(params)[:feat]
    pt_hi, pt_lo = split(turned_params)
    pt_hi = pt_hi.astype(F32)
    pt_lo = pt_lo.astype(F32)
    pt_stack = jnp.concatenate([pt_hi, pt_lo, pt_hi, pt_lo], axis=1).astype(BF16)
    raw_four = jnp.concatenate([raw_hi, raw_hi, raw_lo, raw_lo], axis=0).astype(BF16)
    grad_hidden = dot(pt_stack, raw_four) * cos_buf[...]
    gh_hi, gh_lo = split(grad_hidden)
    gh_stack = jnp.concatenate([gh_hi, gh_lo], axis=0)
    gb_all = dot_lanes(gh_stack, basis_ref[0 : 2 * BAND, :])
    gb_all = gb_all[:feat] + gb_all[feat:]
    gb = (gb_all[:, :BAND] + gb_all[:, BAND : 2 * BAND]) * math.sqrt(
        feat / (seq_total * tp_chans)
    )
    share = feat // ctx_size
    for target in range(ctx_size):
        part_buf[target] = gb[target * share : (target + 1) * share]
    all_others(lambda ctx, tp: push(part_buf.at[ctx], part_in.at[my_id], 5, ctx, tp))
    part_in[my_id] = part_buf[me]

    settle(part_in, recv_sems.at[5], all_size - 1)
    sum_buf[...] = jnp.sum(part_in[...], axis=0)
    others(lambda peer: push(sum_buf, sum_in.at[me], 6, peer, my_tp))

    gp_in[me] = gp_buf[...]
    sum_in[me] = sum_buf[...]
    mq_back[me] = mq_send[me]
    kv_back[me] = kv_send[me]
    settle(mq_back, recv_sems.at[2], ctx_size - 1)
    mq_out[...] = mq_back[...]
    settle(kv_back, recv_sems.at[3], ctx_size - 1)
    kv_out[...] = kv_back[...]
    settle(gp_in, recv_sems.at[4], ctx_size - 1)
    proj_out[...] = gp_in[...]
    settle(sum_in, recv_sems.at[6], ctx_size - 1)
    for source in range(ctx_size):
        basis_out[source * share : (source + 1) * share, :] = sum_in[source][:, :emb]

    settle(kv_in, send_sems.at[0], ctx_size - 1)
    settle(qg_in, send_sems.at[1], ctx_size - 1)
    settle(mq_back, send_sems.at[2], ctx_size - 1)
    settle(kv_back, send_sems.at[3], ctx_size - 1)
    settle(gp_in, send_sems.at[4], ctx_size - 1)
    settle(part_in, send_sems.at[5], all_size - 1)
    settle(sum_in, send_sems.at[6], ctx_size - 1)


def on_device(
    tables,
    query_in,
    key_in,
    value_in,
    short_kernel,
    basis_weight,
    basis_bias,
    filter_proj,
    decay_rate,
    skip_gain,
    grad_out,
):
    ctx_size = lax.axis_size("ctx")
    tp_size = lax.axis_size("tp")
    chan_local, num_tok = query_in.shape
    seq_total = num_tok * ctx_size
    chans = chan_local // ctx_size
    taps = short_kernel.shape[2]
    feat, emb = basis_weight.shape
    folds = num_tok // LANES
    slab = folds * chans
    blocks = seq_total // LANES
    rows = blocks * chans

    def packed(first, second):
        both = jnp.stack([first, second]).reshape(2, ctx_size, chans, folds, LANES)
        return both.transpose(1, 0, 3, 2, 4).reshape(ctx_size, 2, slab, LANES)

    def unpacked(both):
        wide = both.reshape(ctx_size, 2, folds, chans, LANES).transpose(1, 0, 3, 2, 4)
        wide = wide.reshape(2, chan_local, num_tok)
        return wide[0], wide[1]

    energy = jnp.expm1(-2.0 * decay_rate) / jnp.expm1(-2.0 * decay_rate / seq_total)
    params = jnp.concatenate(
        [
            filter_proj,
            short_kernel[0],
            short_kernel[1],
            short_kernel[2],
            decay_rate[:, None],
            (1.0 / jnp.sqrt(energy))[:, None],
            skip_gain[:, None],
        ],
        axis=1,
    )
    params = jnp.pad(params, ((0, 0), (0, LANES - params.shape[1])))
    params = params.reshape(ctx_size, chans, LANES)
    params = jnp.tile(params, (1, 8 // chans, 1))
    weight = jnp.concatenate([basis_weight, basis_bias[:, None]], axis=1)
    weight = jnp.pad(weight, ((0, 0), (0, BAND - emb - 1)))
    weight = jnp.pad(jnp.tile(weight, (1, 6)), ((0, 0), (0, 256 - 6 * BAND)))
    share = feat // ctx_size
    all_size = ctx_size * tp_size
    slabs = (ctx_size, 2, slab, LANES)
    dims = (ctx_size, tp_size, chans, seq_total, taps, feat, emb, chan_local * tp_size)
    vmem = pl.BlockSpec(memory_space=pltpu.VMEM)
    mq, kv, grad_proj, grad_basis = pl.pallas_call(
        functools.partial(mixer_kernel, dims),
        out_shape=(
            jax.ShapeDtypeStruct(slabs, BF16),
            jax.ShapeDtypeStruct(slabs, BF16),
            jax.ShapeDtypeStruct((ctx_size, chans, feat), F32),
            jax.ShapeDtypeStruct((feat, emb), F32),
        ),
        in_specs=[vmem] * (4 + len(tables)),
        out_specs=(vmem, vmem, vmem, vmem),
        scratch_shapes=[
            pltpu.VMEM(slabs, BF16),
            pltpu.VMEM(slabs, BF16),
            pltpu.VMEM(slabs, BF16),
            pltpu.VMEM(slabs, BF16),
            pltpu.VMEM(slabs, BF16),
            pltpu.VMEM(slabs, BF16),
            pltpu.VMEM((2 * feat, seq_total), BF16),
            pltpu.VMEM((feat, seq_total), F32),
            pltpu.VMEM((rows, LANES), F32),
            pltpu.VMEM((rows, LANES), F32),
            pltpu.VMEM((ctx_size, share, BAND), F32),
            pltpu.VMEM((all_size, share, BAND), F32),
            pltpu.VMEM((share, BAND), F32),
            pltpu.VMEM((ctx_size, share, BAND), F32),
            pltpu.VMEM((chans, feat), F32),
            pltpu.VMEM((ctx_size, chans, feat), F32),
            pltpu.SemaphoreType.DMA((7,)),
            pltpu.SemaphoreType.DMA((7,)),
        ],
        compiler_params=pltpu.CompilerParams(
            collective_id=0, has_side_effects=True, vmem_limit_bytes=56 * 1024 * 1024
        ),
    )(packed(key_in, value_in), packed(query_in, grad_out), params, weight, *tables)
    mixed, grad_query = unpacked(mq)
    grad_key, grad_value = unpacked(kv)
    return (
        mixed,
        grad_query,
        grad_key,
        grad_value,
        grad_proj.reshape(chan_local, feat),
        grad_basis,
    )


def solution(mesh):
    ctx_size = mesh.shape["ctx"]

    def whole(*args):
        chans = args[0].shape[0] // mesh.shape["tp"] // ctx_size
        num_freq = (args[4].shape[1] - 1) // 2
        tables = constant_tables(args[0].shape[1], chans, num_freq)
        tables = tuple(jnp.asarray(table) for table in tables)
        return jax.shard_map(
            on_device,
            mesh=mesh,
            in_specs=(
                (P(),) * len(tables),
                P("tp", "ctx"),
                P("tp", "ctx"),
                P("tp", "ctx"),
                P(None, "tp", None),
                P(),
                P(),
                P("tp", None),
                P("tp"),
                P("tp"),
                P("tp", "ctx"),
            ),
            out_specs=(
                P("tp", "ctx"),
                P("tp", "ctx"),
                P("tp", "ctx"),
                P("tp", "ctx"),
                P("tp", None),
                P(),
            ),
            check_vma=False,
        )(tables, *args)

    return whole
```

```python
import functools
import math

import jax
import jax.numpy as jnp
import ml_dtypes
import numpy as np
from jax import lax
from jax.experimental import pallas as pl
from jax.experimental.pallas import tpu as pltpu
from jax.sharding import PartitionSpec as P

MESH = pl.DeviceIdType.MESH
BF16 = jnp.bfloat16
F32 = jnp.float32
LANES = 128
BAND = 40


def halves(table):
    high = table.astype(ml_dtypes.bfloat16)
    low = (table - high.astype(np.float64)).astype(ml_dtypes.bfloat16)
    return high, low


def constant_tables(seq_total, chans, num_freq):
    blocks = seq_total // LANES
    kept = blocks + 1
    period = 2 * blocks
    spec_rows = -(-kept * chans // 8) * 8
    eye = np.eye(chans)
    k1 = np.arange(kept)
    n1 = np.arange(blocks)
    n2 = np.arange(LANES)
    turn = 2.0 * np.pi * ((k1[:, None] * n1[None, :]) % period) / period
    fwd = np.zeros((2, spec_rows, blocks * chans))
    fwd[0, : kept * chans] = np.kron(np.cos(turn), eye)
    fwd[1, : kept * chans] = np.kron(-np.sin(turn), eye)
    weight = np.where((k1 == 0) | (k1 == blocks), 1.0, 2.0)[:, None] / (2.0 * seq_total)
    back = np.zeros((2, spec_rows, blocks * chans))
    back[0, : kept * chans] = np.kron(weight * np.cos(turn), eye)
    back[1, : kept * chans] = np.kron(-weight * np.sin(turn), eye)
    back = back.reshape(2 * spec_rows, blocks * chans)
    fwd = fwd.reshape(2 * spec_rows, blocks * chans)
    if chans % 8 == 0:
        used = np.r_[0:spec_rows, spec_rows + chans : 2 * spec_rows - chans]
        back = back[used]
        fwd = fwd[used]
    back = back.T.copy()
    twist = 2.0 * np.pi * ((k1[:, None] * n2[None, :]) % (2 * seq_total)) / (2 * seq_total)
    twiddle = np.zeros((2, spec_rows, LANES))
    twiddle[0, : kept * chans] = np.repeat(np.cos(twist), chans, axis=0)
    twiddle[1, : kept * chans] = np.repeat(-np.sin(twist), chans, axis=0)
    small = 2.0 * np.pi * ((n2[:, None] * n2[None, :]) % LANES) / LANES
    cos, sin = np.cos(small), np.sin(small)
    inner = np.block([[cos, -sin], [sin, cos]])
    inner_back = np.block([[cos, sin], [-sin, cos]])
    positions = np.arange(seq_total)
    basis = np.zeros((BAND, seq_total))
    basis[0] = positions / seq_total
    for harmonic in range(1, num_freq + 1):
        angles = 2.0 * np.pi * ((harmonic * positions) % seq_total) / seq_total
        basis[2 * harmonic - 1] = np.cos(angles)
        basis[2 * harmonic] = np.sin(angles)
    basis[2 * num_freq + 1] = 1.0
    first = basis.astype(ml_dtypes.bfloat16)
    rest = basis - first.astype(np.float64)
    second = rest.astype(ml_dtypes.bfloat16)
    third = (rest - second.astype(np.float64)).astype(ml_dtypes.bfloat16)
    rim = np.zeros((16, seq_total), ml_dtypes.bfloat16)
    basis_table = np.concatenate([first, second, third, first, second, first, rim])
    return (
        basis_table,
        *halves(fwd),
        *halves(back),
        *halves(inner),
        *halves(inner_back),
        twiddle.astype(np.float32),
    )


def dot(left, right):
    return jnp.dot(left, right, preferred_element_type=F32)


def dot_lanes(left, right):
    return lax.dot_general(left, right, (((1,), (1,)), ((), ())), preferred_element_type=F32)


def split(value):
    high = value.astype(BF16)
    return high, (value - high.astype(F32)).astype(BF16)


def sine_cosine(angle):
    quarter = jnp.floor(angle * (2.0 / math.pi) + 0.5)
    rest = angle - quarter * 1.5703125
    rest = rest - quarter * 4.837512969970703125e-4
    rest = rest - quarter * 7.54978995489188216e-8
    square = rest * rest
    sine = rest + rest * square * (
        -1.6666654611e-1 + square * (8.3321608736e-3 + square * -1.9515295891e-4)
    )
    cosine = (
        1.0
        - 0.5 * square
        + square
        * square
        * (4.166664568298827e-2 + square * (-1.388731625493765e-3 + square * 2.443315711809948e-5))
    )
    turns = quarter.astype(jnp.int32)
    odd = (turns & 1) == 1
    sin_out = jnp.where(odd, cosine, sine)
    cos_out = jnp.where(odd, sine, cosine)
    sin_out = jnp.where((turns & 2) == 2, -sin_out, sin_out)
    cos_out = jnp.where(((turns + 1) & 2) == 2, -cos_out, cos_out)
    return sin_out, cos_out


def mixer_kernel(
    dims,
    query_ref,
    key_ref,
    value_ref,
    grad_ref,
    taps_ref,
    weight_ref,
    bias_ref,
    proj_ref,
    decay_ref,
    skip_ref,
    basis_hbm,
    fwd_hi_hbm,
    fwd_lo_hbm,
    back_hi_hbm,
    back_lo_hbm,
    inner_hi_hbm,
    inner_lo_hbm,
    inv_hi_hbm,
    inv_lo_hbm,
    twiddle_hbm,
    mq_out,
    kv_out,
    proj_out,
    basis_out,
    basis_ref,
    fwd_hi,
    fwd_lo,
    back_hi,
    back_lo,
    inner_hi,
    inner_lo,
    inv_hi,
    inv_lo,
    twiddle_ref,
    kv_ref,
    qg_ref,
    par_buf,
    turn_buf,
    wide_buf,
    kv_in,
    qg_in,
    mq_send,
    kv_send,
    mq_back,
    kv_back,
    act_buf,
    cos_buf,
    filt_buf,
    rows_buf,
    part_buf,
    part_in,
    sum_buf,
    sum_in,
    gp_buf,
    gp_in,
    send_sems,
    recv_sems,
    table_sems,
):
    ctx_size, tp_size, chans, seq_total, taps, feat, emb, tp_chans = dims
    me = lax.axis_index("ctx")
    my_tp = lax.axis_index("tp")
    blocks = seq_total // LANES
    rows = blocks * chans
    spec_rows = twiddle_ref.shape[1]
    slab = kv_ref.shape[2]
    all_size = ctx_size * tp_size
    my_id = my_tp * ctx_size + me
    chunk = 512

    def others(body):
        def step(offset, carry):
            body(lax.rem(me + offset, ctx_size))
            return carry

        lax.fori_loop(1, ctx_size, step, 0)

    def all_others(body):
        def step(offset, carry):
            other = lax.rem(my_id + offset, all_size)
            body(lax.rem(other, ctx_size), other // ctx_size)
            return carry

        lax.fori_loop(1, all_size, step, 0)

    barrier = pltpu.get_barrier_semaphore()

    def greet(ctx, tp):
        pl.semaphore_signal(
            barrier, inc=1, device_id={"ctx": ctx, "tp": tp}, device_id_type=MESH
        )

    all_others(greet)

    loads = [
        pltpu.make_async_copy(source, target, table_sems.at[index])
        for index, (source, target) in enumerate(
            [
                (basis_hbm, basis_ref),
                (fwd_hi_hbm, fwd_hi),
                (fwd_lo_hbm, fwd_lo),
                (inner_hi_hbm, inner_hi),
                (inner_lo_hbm, inner_lo),
                (twiddle_hbm, twiddle_ref),
                (inv_hi_hbm, inv_hi),
                (inv_lo_hbm, inv_lo),
                (back_hi_hbm, back_hi),
                (back_lo_hbm, back_lo),
            ]
        )
    ]
    for load in loads:
        load.start()

    def pack(source, target, index):
        wide = source[...].astype(F32)
        for other in range(ctx_size):
            target[other, index] = jnp.concatenate(
                [
                    wide[other * chans : (other + 1) * chans, fold * LANES : (fold + 1) * LANES]
                    for fold in range(slab // chans)
                ],
                axis=0,
            ).astype(BF16)

    pack(key_ref, kv_ref, 0)
    pack(value_ref, kv_ref, 1)
    pack(query_ref, qg_ref, 0)
    pack(grad_ref, qg_ref, 1)
    pl.semaphore_wait(barrier, all_size - 1)

    def push(src, dst, lane, ctx, tp):
        pltpu.make_async_remote_copy(
            src_ref=src,
            dst_ref=dst,
            send_sem=send_sems.at[lane],
            recv_sem=recv_sems.at[lane],
            device_id={"ctx": ctx, "tp": tp},
            device_id_type=MESH,
        ).start()

    def settle(ref, sem, count):
        part = ref.at[pl.ds(0, count)]
        pltpu.make_async_copy(part, part, sem).wait()

    others(lambda peer: push(kv_ref.at[peer], kv_in.at[me], 0, peer, my_tp))
    others(lambda peer: push(qg_ref.at[peer], qg_in.at[me], 1, peer, my_tp))
    kv_in[me] = kv_ref[me]
    qg_in[me] = qg_ref[me]

    def expm1(value):
        series = 1.0 + value * (1.0 / 12.0)
        for order in range(11, 1, -1):
            series = 1.0 + value * series * (1.0 / order)
        return jnp.where(value > -0.5, value * series, jnp.exp(value) - 1.0)

    rates = decay_ref[...]
    energy = expm1(-2.0 * rates) / expm1(-2.0 * rates / seq_total)
    after = feat + 3 * taps
    par_buf[...] = jnp.zeros_like(par_buf)
    par_buf[0:feat] = proj_ref[...]
    for which in range(3):
        par_buf[feat + which * taps : feat + (which + 1) * taps] = taps_ref[which]
    par_buf[after : after + 1] = rates
    par_buf[after + 1 : after + 2] = 1.0 / jnp.sqrt(energy)
    par_buf[after + 2 : after + 3] = skip_ref[...]
    turn_buf[...] = jnp.transpose(par_buf[...])
    params = turn_buf[pl.ds(pl.multiple_of(me * chans, chans), chans), :]
    if chans < 8:
        params = jnp.concatenate([params] * (8 // chans), axis=0)

    def column(index):
        wide = jnp.broadcast_to(params[:, index : index + 1], (8, LANES))
        return jnp.concatenate([wide] * (rows // 8), axis=0)

    tap_at = feat
    decay = column(after)
    inv_energy = column(after + 1)
    skip = column(after + 2)

    lane_ids = lax.broadcasted_iota(jnp.int32, (rows, LANES), 1)
    row_ids = lax.broadcasted_iota(jnp.int32, (rows, LANES), 0)
    positions = ((row_ids // chans) * LANES + lane_ids).astype(F32)
    envelope = jnp.exp(-(decay * positions) / seq_total) * inv_energy

    wide_buf[...] = jnp.zeros_like(wide_buf)
    wide_buf[0:emb, 0:feat] = weight_ref[...]
    wide_buf[emb : emb + 1, 0:feat] = bias_ref[...]
    weight = jnp.concatenate([wide_buf[...]] * 6 + [jnp.zeros((16, LANES), F32)], axis=0)
    weight = jnp.transpose(weight)[0:feat]
    w_one = weight.astype(BF16)
    w_rest = weight - w_one.astype(F32)
    w_two = w_rest.astype(BF16)
    w_three = (w_rest - w_two.astype(F32)).astype(BF16)
    place = lax.broadcasted_iota(jnp.int32, weight.shape, 1)
    w_stack = jnp.where(
        place < 3 * BAND,
        w_one.astype(F32),
        jnp.where(place < 5 * BAND, w_two.astype(F32), w_three.astype(F32)),
    ).astype(BF16)

    own_proj = params[:, :feat]
    proj_hi, proj_lo = split(own_proj)
    proj_hi = proj_hi.astype(F32)
    proj_lo = proj_lo.astype(F32)
    proj_stack = jnp.concatenate(
        [
            jnp.concatenate([proj_hi, proj_hi], axis=1),
            jnp.concatenate([proj_lo, proj_lo], axis=1),
        ],
        axis=0,
    ).astype(BF16)

    def filter_step(index, carry):
        start = pl.multiple_of(index * chunk, chunk)
        here = pl.ds(start, chunk)
        hidden = dot(w_stack, basis_ref[:, here])
        act, cosine = sine_cosine(hidden)
        cos_buf[:, here] = cosine
        act_hi, act_lo = split(act)
        act_buf[0:feat, here] = act_hi
        act_buf[feat : 2 * feat, here] = act_lo
        both = dot(proj_stack, act_buf[:, here])
        piece = both[0:8] + both[8:16]
        for block in range(chunk // LANES):
            at = pl.multiple_of((index * (chunk // LANES) + block) * chans, chans)
            filt_buf[pl.ds(at, chans), :] = piece[
                0:chans, block * LANES : (block + 1) * LANES
            ]
        return carry

    loads[0].wait()
    lax.fori_loop(0, seq_total // chunk, filter_step, 0)
    filt = (filt_buf[...] * envelope).astype(BF16)

    blank = jnp.zeros((chans, LANES), F32)

    def spectrum(signal):
        outer = dot(fwd_hi[...], signal) + dot(fwd_lo[...], signal)
        out_re, out_im = outer[:spec_rows], outer[spec_rows:]
        if chans % 8 == 0:
            out_im = jnp.concatenate([blank, out_im, blank], axis=0)
        tw_re, tw_im = twiddle_ref[0], twiddle_ref[1]
        turned = jnp.concatenate(
            [out_re * tw_re - out_im * tw_im, out_re * tw_im + out_im * tw_re], axis=1
        )
        high, low = split(turned)
        spec = dot(high, inner_hi[...]) + dot(high, inner_lo[...]) + dot(low, inner_hi[...])
        return spec[:, :LANES], spec[:, LANES:]

    def restore(spec_re, spec_im):
        high, low = split(jnp.concatenate([spec_re, spec_im], axis=1))
        section = dot(high, inv_hi[...]) + dot(high, inv_lo[...]) + dot(low, inv_hi[...])
        sec_re, sec_im = section[:, :LANES], section[:, LANES:]
        tw_re, tw_im = twiddle_ref[0], twiddle_ref[1]
        turn_im = sec_im * tw_re - sec_re * tw_im
        if chans % 8 == 0:
            turn_im = turn_im[chans : spec_rows - chans]
        turned = jnp.concatenate([sec_re * tw_re + sec_im * tw_im, turn_im], axis=0)
        high, low = split(turned)
        return dot(back_hi[...], high) + dot(back_lo[...], high) + dot(back_hi[...], low)

    def to_rows(ref, index):
        if slab % 16 == 0:
            return ref[:, index].reshape(rows, LANES).astype(F32)
        for source in range(ctx_size):
            rows_buf[source * slab : (source + 1) * slab, :] = ref[source, index].astype(F32)
        return rows_buf[...]

    def from_rows(ref, index, value):
        if slab % 16 == 0:
            ref[:, index] = value.reshape(ctx_size, slab, LANES)
        else:
            rows_buf[...] = value.astype(F32)
            for target in range(ctx_size):
                ref[target, index] = rows_buf[target * slab : (target + 1) * slab, :].astype(BF16)

    def down(value):
        if chans % 8 == 0:
            return jnp.concatenate([blank, value[: rows - chans]], axis=0)
        return jnp.where(row_ids < chans, 0.0, pltpu.roll(value, chans, 0))

    def up(value):
        if chans % 8 == 0:
            return jnp.concatenate([value[chans:], blank], axis=0)
        return jnp.where(row_ids >= rows - chans, 0.0, pltpu.roll(value, rows - chans, 0))

    def featurize(signal, which):
        result = column(tap_at + which * taps) * signal
        for offset in range(1, taps):
            turned = pltpu.roll(signal, offset, 1)
            shifted = jnp.where(lane_ids < offset, down(turned), turned)
            result = result + column(tap_at + which * taps + offset) * shifted
        return result

    def featurize_back(signal, which):
        result = column(tap_at + which * taps) * signal
        for offset in range(1, taps):
            turned = pltpu.roll(signal, LANES - offset, 1)
            shifted = jnp.where(lane_ids >= LANES - offset, up(turned), turned)
            result = result + column(tap_at + which * taps + offset) * shifted
        return result

    for load in loads[1:]:
        load.wait()
    filt_re, filt_im = spectrum(filt)

    settle(kv_in, recv_sems.at[0], ctx_size - 1)
    key_feat = featurize(to_rows(kv_in, 0), 1)
    value_feat = featurize(to_rows(kv_in, 1), 2)
    carried = (key_feat * value_feat).astype(BF16)
    carried_re, carried_im = spectrum(carried)

    long_out = restore(
        filt_re * carried_re - filt_im * carried_im, filt_re * carried_im + filt_im * carried_re
    )
    long_out = (long_out + skip * carried.astype(F32)).astype(BF16).astype(F32)

    settle(qg_in, recv_sems.at[1], ctx_size - 1)
    query_feat = featurize(to_rows(qg_in, 0), 0)
    grad_wide = to_rows(qg_in, 1)
    from_rows(mq_send, 0, (query_feat * long_out).astype(BF16))
    grad_query_feat = (grad_wide * long_out).astype(BF16).astype(F32)
    from_rows(mq_send, 1, featurize_back(grad_query_feat, 0).astype(BF16))
    others(lambda peer: push(mq_send.at[peer], mq_back.at[me], 2, peer, my_tp))

    grad_long = (grad_wide * query_feat).astype(BF16)
    grad_re, grad_im = spectrum(grad_long)

    filter_grad = restore(
        carried_re * grad_re + carried_im * grad_im, carried_re * grad_im - carried_im * grad_re
    )
    grad_raw = filter_grad.astype(BF16).astype(F32) * envelope
    if chans % 8 == 0:
        raw_wide = jnp.concatenate(
            [grad_raw[block * chans : (block + 1) * chans] for block in range(blocks)], axis=1
        )
    else:
        rows_buf[...] = grad_raw
        raw_wide = jnp.concatenate(
            [
                jnp.concatenate(
                    [
                        rows_buf[block * chans : (block + 1) * chans, :],
                        jnp.zeros((8 - chans, LANES), F32),
                    ],
                    axis=0,
                )
                for block in range(blocks)
            ],
            axis=1,
        )
    raw_hi, raw_lo = split(raw_wide)
    raw_hi = raw_hi.astype(F32)
    raw_lo = raw_lo.astype(F32)
    raw_two = jnp.concatenate([raw_hi, raw_lo], axis=0).astype(BF16)
    gp_all = dot_lanes(raw_two, act_buf[...])
    gp_all = gp_all[0:8] + gp_all[8:16]
    gp = gp_all + pltpu.roll(gp_all, feat, 1)
    gp_buf[...] = gp[0:chans] * (1.0 / math.sqrt(seq_total))
    others(lambda peer: push(gp_buf, gp_in.at[me], 4, peer, my_tp))

    turned_params = jnp.transpose(params)[:feat]
    pt_hi, pt_lo = split(turned_params)
    pt_hi = pt_hi.astype(F32)
    pt_lo = pt_lo.astype(F32)
    pt_stack = jnp.concatenate([pt_hi, pt_lo, pt_hi, pt_lo], axis=1).astype(BF16)
    raw_four = jnp.concatenate([raw_hi, raw_hi, raw_lo, raw_lo], axis=0).astype(BF16)
    grad_hidden = dot(pt_stack, raw_four) * cos_buf[...]
    gh_hi, gh_lo = split(grad_hidden)
    gh_stack = jnp.concatenate([gh_hi, gh_lo], axis=0)
    gb_all = dot_lanes(gh_stack, basis_ref[0:LANES, :])
    gb_all = gb_all[:feat] + gb_all[feat:]
    gb = (gb_all + pltpu.roll(gb_all, LANES - BAND, 1)) * math.sqrt(
        feat / (seq_total * tp_chans)
    )
    share = feat // ctx_size
    for target in range(ctx_size):
        part_buf[target] = gb[target * share : (target + 1) * share]
    all_others(lambda ctx, tp: push(part_buf.at[ctx], part_in.at[my_id], 5, ctx, tp))
    part_in[my_id] = part_buf[me]

    carried_grad = restore(
        filt_re * grad_re + filt_im * grad_im, filt_re * grad_im - filt_im * grad_re
    )
    carried_grad = (carried_grad + skip * grad_long.astype(F32)).astype(BF16).astype(F32)
    grad_key_feat = (carried_grad * value_feat).astype(BF16).astype(F32)
    grad_value_feat = (carried_grad * key_feat).astype(BF16).astype(F32)
    from_rows(kv_send, 0, featurize_back(grad_key_feat, 1).astype(BF16))
    from_rows(kv_send, 1, featurize_back(grad_value_feat, 2).astype(BF16))
    others(lambda peer: push(kv_send.at[peer], kv_back.at[me], 3, peer, my_tp))

    settle(part_in, recv_sems.at[5], all_size - 1)
    sum_buf[...] = jnp.sum(part_in[...], axis=0)
    others(lambda peer: push(sum_buf, sum_in.at[me], 6, peer, my_tp))

    gp_in[me] = gp_buf[...]
    sum_in[me] = sum_buf[...]
    mq_back[me] = mq_send[me]
    kv_back[me] = kv_send[me]
    settle(mq_back, recv_sems.at[2], ctx_size - 1)
    mq_out[...] = mq_back[...]
    settle(kv_back, recv_sems.at[3], ctx_size - 1)
    kv_out[...] = kv_back[...]
    settle(gp_in, recv_sems.at[4], ctx_size - 1)
    proj_out[...] = gp_in[...]
    settle(sum_in, recv_sems.at[6], ctx_size - 1)
    basis_out[...] = sum_in[...]

    settle(kv_in, send_sems.at[0], ctx_size - 1)
    settle(qg_in, send_sems.at[1], ctx_size - 1)
    settle(mq_back, send_sems.at[2], ctx_size - 1)
    settle(kv_back, send_sems.at[3], ctx_size - 1)
    settle(gp_in, send_sems.at[4], ctx_size - 1)
    settle(part_in, send_sems.at[5], all_size - 1)
    settle(sum_in, send_sems.at[6], ctx_size - 1)


def unpack_kernel(
    dims,
    mq_ref,
    kv_ref,
    proj_ref,
    basis_ref,
    mixed_out,
    query_out,
    key_out,
    value_out,
    proj_out,
    basis_out,
):
    ctx_size, chans, folds, share = dims
    feat = ctx_size * share
    group = max(1, 16 // chans)
    for source, index, target in (
        (mq_ref, 0, mixed_out),
        (mq_ref, 1, query_out),
        (kv_ref, 0, key_out),
        (kv_ref, 1, value_out),
    ):
        for first in range(0, ctx_size, group):
            pieces = [source[first + other, index].astype(F32) for other in range(group)]
            for fold in range(folds):
                target[
                    first * chans : (first + group) * chans, fold * LANES : (fold + 1) * LANES
                ] = jnp.concatenate(
                    [piece[fold * chans : (fold + 1) * chans] for piece in pieces], axis=0
                ).astype(BF16)
    proj = jnp.concatenate([proj_ref[source] for source in range(ctx_size)], axis=0)
    proj_out[...] = jnp.transpose(proj)[:feat]
    basis = jnp.concatenate([basis_ref[source] for source in range(ctx_size)], axis=0)
    basis_out[...] = jnp.transpose(basis)[: basis_out.shape[0]]


def on_device(
    tables,
    query_in,
    key_in,
    value_in,
    short_kernel,
    basis_weight,
    basis_bias,
    filter_proj,
    decay_rate,
    skip_gain,
    grad_out,
):
    ctx_size = lax.axis_size("ctx")
    tp_size = lax.axis_size("tp")
    chan_local, num_tok = query_in.shape
    seq_total = num_tok * ctx_size
    chans = chan_local // ctx_size
    taps = short_kernel.shape[2]
    feat, emb = basis_weight.shape
    folds = num_tok // LANES
    slab = folds * chans
    blocks = seq_total // LANES
    rows = blocks * chans

    share = feat // ctx_size
    all_size = ctx_size * tp_size
    slabs = (ctx_size, 2, slab, LANES)
    dims = (ctx_size, tp_size, chans, seq_total, taps, feat, emb, chan_local * tp_size)
    vmem = pl.BlockSpec(memory_space=pltpu.VMEM)
    anywhere = pl.BlockSpec(memory_space=pl.ANY)
    landed = pl.pallas_call(
        functools.partial(mixer_kernel, dims),
        out_shape=(
            jax.ShapeDtypeStruct(slabs, BF16),
            jax.ShapeDtypeStruct(slabs, BF16),
            jax.ShapeDtypeStruct((ctx_size, chans, LANES), F32),
            jax.ShapeDtypeStruct((ctx_size, share, LANES), F32),
        ),
        in_specs=[vmem] * 10 + [anywhere] * len(tables),
        out_specs=(vmem, vmem, vmem, vmem),
        scratch_shapes=[pltpu.VMEM(table.shape, table.dtype) for table in tables]
        + [
            pltpu.VMEM(slabs, BF16),
            pltpu.VMEM(slabs, BF16),
            pltpu.VMEM((LANES, chan_local), F32),
            pltpu.VMEM((chan_local, LANES), F32),
            pltpu.VMEM((BAND, LANES), F32),
            pltpu.VMEM(slabs, BF16),
            pltpu.VMEM(slabs, BF16),
            pltpu.VMEM(slabs, BF16),
            pltpu.VMEM(slabs, BF16),
            pltpu.VMEM(slabs, BF16),
            pltpu.VMEM(slabs, BF16),
            pltpu.VMEM((2 * feat, seq_total), BF16),
            pltpu.VMEM((feat, seq_total), F32),
            pltpu.VMEM((rows, LANES), F32),
            pltpu.VMEM((rows, LANES), F32),
            pltpu.VMEM((ctx_size, share, LANES), F32),
            pltpu.VMEM((all_size, share, LANES), F32),
            pltpu.VMEM((share, LANES), F32),
            pltpu.VMEM((ctx_size, share, LANES), F32),
            pltpu.VMEM((chans, LANES), F32),
            pltpu.VMEM((ctx_size, chans, LANES), F32),
            pltpu.SemaphoreType.DMA((7,)),
            pltpu.SemaphoreType.DMA((7,)),
            pltpu.SemaphoreType.DMA((len(tables),)),
        ],
        compiler_params=pltpu.CompilerParams(
            collective_id=0, has_side_effects=True, vmem_limit_bytes=56 * 1024 * 1024
        ),
    )(
        query_in,
        key_in,
        value_in,
        grad_out,
        short_kernel.transpose(0, 2, 1),
        basis_weight.T,
        basis_bias[None, :],
        filter_proj.T,
        decay_rate[None, :],
        skip_gain[None, :],
        *tables,
    )
    block = jax.ShapeDtypeStruct((chan_local, num_tok), BF16)
    mixed, grad_query, grad_key, grad_value, proj_turned, basis_turned = pl.pallas_call(
        functools.partial(unpack_kernel, (ctx_size, chans, folds, share)),
        out_shape=(
            block,
            block,
            block,
            block,
            jax.ShapeDtypeStruct((feat, chan_local), F32),
            jax.ShapeDtypeStruct((emb, feat), F32),
        ),
        in_specs=[vmem] * 4,
        out_specs=(vmem,) * 6,
    )(*landed)
    return (mixed, grad_query, grad_key, grad_value, proj_turned.T, basis_turned.T)


def solution(mesh):
    ctx_size = mesh.shape["ctx"]

    def whole(*args):
        chans = args[0].shape[0] // mesh.shape["tp"] // ctx_size
        num_freq = (args[4].shape[1] - 1) // 2
        tables = constant_tables(args[0].shape[1], chans, num_freq)
        tables = tuple(jnp.asarray(table) for table in tables)
        return jax.shard_map(
            on_device,
            mesh=mesh,
            in_specs=(
                (P(),) * len(tables),
                P("tp", "ctx"),
                P("tp", "ctx"),
                P("tp", "ctx"),
                P(None, "tp", None),
                P(),
                P(),
                P("tp", None),
                P("tp"),
                P("tp"),
                P("tp", "ctx"),
            ),
            out_specs=(
                P("tp", "ctx"),
                P("tp", "ctx"),
                P("tp", "ctx"),
                P("tp", "ctx"),
                P("tp", None),
                P(),
            ),
            check_vma=False,
        )(tables, *args)

    return whole
```

```python
import functools
import math

import jax
import jax.numpy as jnp
import ml_dtypes
import numpy as np
from jax import lax
from jax.experimental import pallas as pl
from jax.experimental.pallas import tpu as pltpu
from jax.sharding import PartitionSpec as P

MESH = pl.DeviceIdType.MESH
BF16 = jnp.bfloat16
F32 = jnp.float32
LANES = 128
BAND = 40


def halves(table):
    high = table.astype(ml_dtypes.bfloat16)
    low = (table - high.astype(np.float64)).astype(ml_dtypes.bfloat16)
    return high, low


def constant_tables(seq_total, chans, num_freq):
    blocks = seq_total // LANES
    kept = blocks + 1
    period = 2 * blocks
    spec_rows = -(-kept * chans // 8) * 8
    eye = np.eye(chans)
    k1 = np.arange(kept)
    n1 = np.arange(blocks)
    n2 = np.arange(LANES)
    turn = 2.0 * np.pi * ((k1[:, None] * n1[None, :]) % period) / period
    fwd = np.zeros((2, spec_rows, blocks * chans))
    fwd[0, : kept * chans] = np.kron(np.cos(turn), eye)
    fwd[1, : kept * chans] = np.kron(-np.sin(turn), eye)
    weight = np.where((k1 == 0) | (k1 == blocks), 1.0, 2.0)[:, None] / (2.0 * seq_total)
    back = np.zeros((2, spec_rows, blocks * chans))
    back[0, : kept * chans] = np.kron(weight * np.cos(turn), eye)
    back[1, : kept * chans] = np.kron(-weight * np.sin(turn), eye)
    back = back.reshape(2 * spec_rows, blocks * chans)
    fwd = fwd.reshape(2 * spec_rows, blocks * chans)
    if chans % 8 == 0:
        used = np.r_[0:spec_rows, spec_rows + chans : 2 * spec_rows - chans]
        back = back[used]
        fwd = fwd[used]
    back = back.T.copy()
    twist = 2.0 * np.pi * ((k1[:, None] * n2[None, :]) % (2 * seq_total)) / (2 * seq_total)
    twiddle = np.zeros((2, spec_rows, LANES))
    twiddle[0, : kept * chans] = np.repeat(np.cos(twist), chans, axis=0)
    twiddle[1, : kept * chans] = np.repeat(-np.sin(twist), chans, axis=0)
    small = 2.0 * np.pi * ((n2[:, None] * n2[None, :]) % LANES) / LANES
    cos, sin = np.cos(small), np.sin(small)
    inner = np.block([[cos, -sin], [sin, cos]])
    inner_back = np.block([[cos, sin], [-sin, cos]])
    positions = np.arange(seq_total)
    basis = np.zeros((BAND, seq_total))
    basis[0] = positions / seq_total
    for harmonic in range(1, num_freq + 1):
        angles = 2.0 * np.pi * ((harmonic * positions) % seq_total) / seq_total
        basis[2 * harmonic - 1] = np.cos(angles)
        basis[2 * harmonic] = np.sin(angles)
    basis[2 * num_freq + 1] = 1.0
    first = basis.astype(ml_dtypes.bfloat16)
    rest = basis - first.astype(np.float64)
    second = rest.astype(ml_dtypes.bfloat16)
    third = (rest - second.astype(np.float64)).astype(ml_dtypes.bfloat16)
    rim = np.zeros((16, seq_total), ml_dtypes.bfloat16)
    basis_table = np.concatenate([first, second, third, first, second, first, rim])
    return (
        basis_table,
        *halves(fwd),
        *halves(back),
        *halves(inner),
        *halves(inner_back),
        twiddle.astype(np.float32),
    )


def dot(left, right):
    return jnp.dot(left, right, preferred_element_type=F32)


def dot_lanes(left, right):
    return lax.dot_general(left, right, (((1,), (1,)), ((), ())), preferred_element_type=F32)


def split(value):
    high = value.astype(BF16)
    return high, (value - high.astype(F32)).astype(BF16)


def sine_cosine(angle):
    quarter = jnp.floor(angle * (2.0 / math.pi) + 0.5)
    rest = angle - quarter * 1.5703125
    rest = rest - quarter * 4.837512969970703125e-4
    rest = rest - quarter * 7.54978995489188216e-8
    square = rest * rest
    sine = rest + rest * square * (
        -1.6666654611e-1 + square * (8.3321608736e-3 + square * -1.9515295891e-4)
    )
    cosine = (
        1.0
        - 0.5 * square
        + square
        * square
        * (4.166664568298827e-2 + square * (-1.388731625493765e-3 + square * 2.443315711809948e-5))
    )
    turns = quarter.astype(jnp.int32)
    odd = (turns & 1) == 1
    sin_out = jnp.where(odd, cosine, sine)
    cos_out = jnp.where(odd, sine, cosine)
    sin_out = jnp.where((turns & 2) == 2, -sin_out, sin_out)
    cos_out = jnp.where(((turns + 1) & 2) == 2, -cos_out, cos_out)
    return sin_out, cos_out


def mixer_kernel(
    dims,
    query_ref,
    key_ref,
    value_ref,
    grad_ref,
    taps_ref,
    weight_ref,
    bias_ref,
    proj_ref,
    decay_ref,
    skip_ref,
    basis_hbm,
    fwd_hi_hbm,
    fwd_lo_hbm,
    back_hi_hbm,
    back_lo_hbm,
    inner_hi_hbm,
    inner_lo_hbm,
    inv_hi_hbm,
    inv_lo_hbm,
    twiddle_hbm,
    mq_out,
    kv_out,
    proj_out,
    basis_out,
    basis_ref,
    fwd_hi,
    fwd_lo,
    back_hi,
    back_lo,
    inner_hi,
    inner_lo,
    inv_hi,
    inv_lo,
    twiddle_ref,
    raw_ref,
    par_buf,
    turn_buf,
    wide_buf,
    raw_in,
    mq_send,
    kv_send,
    mq_back,
    kv_back,
    act_buf,
    cos_buf,
    filt_buf,
    rows_buf,
    part_buf,
    part_in,
    half_buf,
    sum_buf,
    sum_in,
    send_sems,
    recv_sems,
    table_sems,
):
    ctx_size, tp_size, chans, seq_total, taps, feat, emb, tp_chans = dims
    me = lax.axis_index("ctx")
    my_tp = lax.axis_index("tp")
    blocks = seq_total // LANES
    rows = blocks * chans
    spec_rows = twiddle_ref.shape[1]
    slab = raw_ref.shape[2]
    chunk = 512

    def around(axis_size, own, body):
        def step(offset, carry):
            other = own + offset
            body(jnp.where(other >= axis_size, other - axis_size, other))
            return carry

        if axis_size <= 16:
            for offset in range(1, axis_size):
                step(offset, 0)
        else:
            lax.fori_loop(1, axis_size, step, 0)

    def others(body):
        around(ctx_size, me, body)

    def tp_others(body):
        around(tp_size, my_tp, body)

    barrier = pltpu.get_barrier_semaphore()

    def greet(ctx, tp):
        pl.semaphore_signal(
            barrier, inc=1, device_id={"ctx": ctx, "tp": tp}, device_id_type=MESH
        )

    others(lambda peer: greet(peer, my_tp))
    tp_others(lambda peer: greet(me, peer))

    loads = [
        pltpu.make_async_copy(source, target, table_sems.at[index])
        for index, (source, target) in enumerate(
            [
                (basis_hbm, basis_ref),
                (fwd_hi_hbm, fwd_hi),
                (fwd_lo_hbm, fwd_lo),
                (inner_hi_hbm, inner_hi),
                (inner_lo_hbm, inner_lo),
                (twiddle_hbm, twiddle_ref),
                (inv_hi_hbm, inv_hi),
                (inv_lo_hbm, inv_lo),
                (back_hi_hbm, back_hi),
                (back_lo_hbm, back_lo),
            ]
        )
    ]
    for load in loads:
        load.start()

    def pack(source, target, index):
        wide = source[...].astype(F32)
        for other in range(ctx_size):
            target[other, index] = jnp.concatenate(
                [
                    wide[other * chans : (other + 1) * chans, fold * LANES : (fold + 1) * LANES]
                    for fold in range(slab // chans)
                ],
                axis=0,
            ).astype(BF16)

    pack(key_ref, raw_ref, 0)
    pack(value_ref, raw_ref, 1)
    pack(query_ref, raw_ref, 2)
    pack(grad_ref, raw_ref, 3)
    pl.semaphore_wait(barrier, ctx_size + tp_size - 2)

    def push(src, dst, lane, ctx, tp):
        pltpu.make_async_remote_copy(
            src_ref=src,
            dst_ref=dst,
            send_sem=send_sems.at[lane],
            recv_sem=recv_sems.at[lane],
            device_id={"ctx": ctx, "tp": tp},
            device_id_type=MESH,
        ).start()

    def settle(ref, sem, count):
        part = ref.at[pl.ds(0, count)]
        pltpu.make_async_copy(part, part, sem).wait()

    others(lambda peer: push(raw_ref.at[peer], raw_in.at[me], 0, peer, my_tp))
    raw_in[me] = raw_ref[me]

    def expm1(value):
        series = 1.0 + value * (1.0 / 12.0)
        for order in range(11, 1, -1):
            series = 1.0 + value * series * (1.0 / order)
        return jnp.where(value > -0.5, value * series, jnp.exp(value) - 1.0)

    rates = decay_ref[...]
    energy = expm1(-2.0 * rates) / expm1(-2.0 * rates / seq_total)
    after = feat + 3 * taps
    par_buf[...] = jnp.zeros_like(par_buf)
    par_buf[0:feat] = proj_ref[...]
    for which in range(3):
        par_buf[feat + which * taps : feat + (which + 1) * taps] = taps_ref[which]
    par_buf[after : after + 1] = rates
    par_buf[after + 1 : after + 2] = 1.0 / jnp.sqrt(energy)
    par_buf[after + 2 : after + 3] = skip_ref[...]
    turn_buf[...] = jnp.transpose(par_buf[...])
    params = turn_buf[pl.ds(pl.multiple_of(me * chans, chans), chans), :]
    if chans < 8:
        params = jnp.concatenate([params] * (8 // chans), axis=0)

    def column(index):
        wide = jnp.broadcast_to(params[:, index : index + 1], (8, LANES))
        return jnp.concatenate([wide] * (rows // 8), axis=0)

    tap_at = feat
    decay = column(after)
    inv_energy = column(after + 1)
    skip = column(after + 2)

    lane_ids = lax.broadcasted_iota(jnp.int32, (rows, LANES), 1)
    row_ids = lax.broadcasted_iota(jnp.int32, (rows, LANES), 0)
    positions = ((row_ids // chans) * LANES + lane_ids).astype(F32)
    envelope = jnp.exp(-(decay * positions) / seq_total) * inv_energy

    wide_buf[...] = jnp.zeros_like(wide_buf)
    wide_buf[0:emb, 0:feat] = weight_ref[...]
    wide_buf[emb : emb + 1, 0:feat] = bias_ref[...]
    weight = jnp.concatenate([wide_buf[...]] * 6 + [jnp.zeros((16, LANES), F32)], axis=0)
    weight = jnp.transpose(weight)[0:feat]
    w_one = weight.astype(BF16)
    w_rest = weight - w_one.astype(F32)
    w_two = w_rest.astype(BF16)
    w_three = (w_rest - w_two.astype(F32)).astype(BF16)
    place = lax.broadcasted_iota(jnp.int32, weight.shape, 1)
    w_stack = jnp.where(
        place < 3 * BAND,
        w_one.astype(F32),
        jnp.where(place < 5 * BAND, w_two.astype(F32), w_three.astype(F32)),
    ).astype(BF16)

    own_proj = params[:, :feat]
    proj_hi, proj_lo = split(own_proj)
    proj_hi = proj_hi.astype(F32)
    proj_lo = proj_lo.astype(F32)
    proj_stack = jnp.concatenate(
        [
            jnp.concatenate([proj_hi, proj_hi], axis=1),
            jnp.concatenate([proj_lo, proj_lo], axis=1),
        ],
        axis=0,
    ).astype(BF16)

    def filter_step(index, carry):
        start = pl.multiple_of(index * chunk, chunk)
        here = pl.ds(start, chunk)
        hidden = dot(w_stack, basis_ref[:, here])
        act, cosine = sine_cosine(hidden)
        cos_buf[:, here] = cosine
        act_hi, act_lo = split(act)
        act_buf[0:feat, here] = act_hi
        act_buf[feat : 2 * feat, here] = act_lo
        both = dot(proj_stack, act_buf[:, here])
        piece = both[0:8] + both[8:16]
        for block in range(chunk // LANES):
            at = pl.multiple_of((index * (chunk // LANES) + block) * chans, chans)
            filt_buf[pl.ds(at, chans), :] = piece[
                0:chans, block * LANES : (block + 1) * LANES
            ]
        return carry

    loads[0].wait()
    lax.fori_loop(0, seq_total // chunk, filter_step, 0)
    filt = (filt_buf[...] * envelope).astype(BF16)

    blank = jnp.zeros((chans, LANES), F32)

    def spectra(signals):
        count = len(signals)
        both = jnp.concatenate(signals, axis=1) if count > 1 else signals[0]
        outer = dot(fwd_hi[...], both) + dot(fwd_lo[...], both)
        tw_re, tw_im = twiddle_ref[0], twiddle_ref[1]
        turned = []
        for index in range(count):
            own = outer[:, index * LANES : (index + 1) * LANES]
            out_re, out_im = own[:spec_rows], own[spec_rows:]
            if chans % 8 == 0:
                out_im = jnp.concatenate([blank, out_im, blank], axis=0)
            turned.append(
                jnp.concatenate(
                    [out_re * tw_re - out_im * tw_im, out_re * tw_im + out_im * tw_re], axis=1
                )
            )
        high, low = split(jnp.concatenate(turned, axis=0) if count > 1 else turned[0])
        spec = dot(high, inner_hi[...]) + dot(high, inner_lo[...]) + dot(low, inner_hi[...])
        return [
            (
                spec[index * spec_rows : (index + 1) * spec_rows, :LANES],
                spec[index * spec_rows : (index + 1) * spec_rows, LANES:],
            )
            for index in range(count)
        ]

    def restore(spec_re, spec_im):
        high, low = split(jnp.concatenate([spec_re, spec_im], axis=1))
        section = dot(high, inv_hi[...]) + dot(high, inv_lo[...]) + dot(low, inv_hi[...])
        sec_re, sec_im = section[:, :LANES], section[:, LANES:]
        tw_re, tw_im = twiddle_ref[0], twiddle_ref[1]
        turn_im = sec_im * tw_re - sec_re * tw_im
        if chans % 8 == 0:
            turn_im = turn_im[chans : spec_rows - chans]
        turned = jnp.concatenate([sec_re * tw_re + sec_im * tw_im, turn_im], axis=0)
        high, low = split(turned)
        pair = dot(back_hi[...], jnp.concatenate([high, low], axis=1))
        return pair[:, :LANES] + pair[:, LANES:] + dot(back_lo[...], high)

    def to_rows(ref, index):
        if slab % 16 == 0:
            return ref[:, index].reshape(rows, LANES).astype(F32)
        for source in range(ctx_size):
            rows_buf[source * slab : (source + 1) * slab, :] = ref[source, index].astype(F32)
        return rows_buf[...]

    def from_rows(ref, index, value):
        if slab % 16 == 0:
            ref[:, index] = value.reshape(ctx_size, slab, LANES)
        else:
            rows_buf[...] = value.astype(F32)
            for target in range(ctx_size):
                ref[target, index] = rows_buf[target * slab : (target + 1) * slab, :].astype(BF16)

    def down(value):
        if chans % 8 == 0:
            return jnp.concatenate([blank, value[: rows - chans]], axis=0)
        return jnp.where(row_ids < chans, 0.0, pltpu.roll(value, chans, 0))

    def up(value):
        if chans % 8 == 0:
            return jnp.concatenate([value[chans:], blank], axis=0)
        return jnp.where(row_ids >= rows - chans, 0.0, pltpu.roll(value, rows - chans, 0))

    def featurize(signal, which):
        result = column(tap_at + which * taps) * signal
        for offset in range(1, taps):
            turned = pltpu.roll(signal, offset, 1)
            shifted = jnp.where(lane_ids < offset, down(turned), turned)
            result = result + column(tap_at + which * taps + offset) * shifted
        return result

    def featurize_back(signal, which):
        result = column(tap_at + which * taps) * signal
        for offset in range(1, taps):
            turned = pltpu.roll(signal, LANES - offset, 1)
            shifted = jnp.where(lane_ids >= LANES - offset, up(turned), turned)
            result = result + column(tap_at + which * taps + offset) * shifted
        return result

    for load in loads[1:]:
        load.wait()
    ((filt_re, filt_im),) = spectra([filt])

    settle(raw_in, recv_sems.at[0], ctx_size - 1)
    key_feat = featurize(to_rows(raw_in, 0), 1)
    value_feat = featurize(to_rows(raw_in, 1), 2)
    query_feat = featurize(to_rows(raw_in, 2), 0)
    grad_wide = to_rows(raw_in, 3)
    carried = (key_feat * value_feat).astype(BF16)
    grad_long = (grad_wide * query_feat).astype(BF16)
    (carried_re, carried_im), (grad_re, grad_im) = spectra([carried, grad_long])

    long_out = restore(
        filt_re * carried_re - filt_im * carried_im, filt_re * carried_im + filt_im * carried_re
    )
    long_out = (long_out + skip * carried.astype(F32)).astype(BF16).astype(F32)

    from_rows(mq_send, 0, (query_feat * long_out).astype(BF16))
    grad_query_feat = (grad_wide * long_out).astype(BF16).astype(F32)
    from_rows(mq_send, 1, featurize_back(grad_query_feat, 0).astype(BF16))
    others(lambda peer: push(mq_send.at[peer], mq_back.at[me], 2, peer, my_tp))

    filter_grad = restore(
        carried_re * grad_re + carried_im * grad_im, carried_re * grad_im - carried_im * grad_re
    )
    grad_raw = filter_grad.astype(BF16).astype(F32) * envelope
    if chans % 8 == 0:
        raw_wide = jnp.concatenate(
            [grad_raw[block * chans : (block + 1) * chans] for block in range(blocks)], axis=1
        )
    else:
        rows_buf[...] = grad_raw
        raw_wide = jnp.concatenate(
            [
                jnp.concatenate(
                    [
                        rows_buf[block * chans : (block + 1) * chans, :],
                        jnp.zeros((8 - chans, LANES), F32),
                    ],
                    axis=0,
                )
                for block in range(blocks)
            ],
            axis=1,
        )
    raw_hi, raw_lo = split(raw_wide)
    raw_hi = raw_hi.astype(F32)
    raw_lo = raw_lo.astype(F32)
    raw_two = jnp.concatenate([raw_hi, raw_lo], axis=0).astype(BF16)
    gp_all = dot_lanes(raw_two, act_buf[...])
    gp_all = gp_all[0:8] + gp_all[8:16]
    gp = gp_all + pltpu.roll(gp_all, feat, 1)
    gp = gp[0:chans] * (1.0 / math.sqrt(seq_total))

    turned_params = jnp.transpose(params)[:feat]
    pt_hi, pt_lo = split(turned_params)
    pt_hi = pt_hi.astype(F32)
    pt_lo = pt_lo.astype(F32)
    pt_stack = jnp.concatenate([pt_hi, pt_lo, pt_hi, pt_lo], axis=1).astype(BF16)
    raw_four = jnp.concatenate([raw_hi, raw_hi, raw_lo, raw_lo], axis=0).astype(BF16)
    grad_hidden = dot(pt_stack, raw_four) * cos_buf[...]
    gh_hi, gh_lo = split(grad_hidden)
    gh_stack = jnp.concatenate([gh_hi, gh_lo], axis=0)
    gb_all = dot_lanes(gh_stack, basis_ref[0:LANES, :])
    gb_all = gb_all[:feat] + gb_all[feat:]
    gb = (gb_all + pltpu.roll(gb_all, LANES - BAND, 1)) * math.sqrt(
        feat / (seq_total * tp_chans)
    )
    share = feat // ctx_size
    for target in range(ctx_size):
        part_buf[target, 0:chans] = gp
        part_buf[target, chans : chans + share] = gb[target * share : (target + 1) * share]
    others(lambda peer: push(part_buf.at[peer], part_in.at[me], 1, peer, my_tp))
    part_in[me] = part_buf[me]

    carried_grad = restore(
        filt_re * grad_re + filt_im * grad_im, filt_re * grad_im - filt_im * grad_re
    )
    carried_grad = (carried_grad + skip * grad_long.astype(F32)).astype(BF16).astype(F32)
    grad_key_feat = (carried_grad * value_feat).astype(BF16).astype(F32)
    grad_value_feat = (carried_grad * key_feat).astype(BF16).astype(F32)
    from_rows(kv_send, 0, featurize_back(grad_key_feat, 1).astype(BF16))
    from_rows(kv_send, 1, featurize_back(grad_value_feat, 2).astype(BF16))
    settle(part_in, recv_sems.at[1], ctx_size - 1)
    half_buf[my_tp] = jnp.sum(part_in[:, chans : chans + share], axis=0)
    tp_others(lambda peer: push(half_buf.at[my_tp], half_buf.at[my_tp], 4, me, peer))
    others(lambda peer: push(kv_send.at[peer], kv_back.at[me], 3, peer, my_tp))

    settle(half_buf, recv_sems.at[4], tp_size - 1)
    sum_buf[...] = jnp.sum(half_buf[...], axis=0)
    others(lambda peer: push(sum_buf, sum_in.at[me], 5, peer, my_tp))
    sum_in[me] = sum_buf[...]
    mq_back[me] = mq_send[me]
    kv_back[me] = kv_send[me]
    proj_out[...] = part_in[:, 0:chans]
    settle(mq_back, recv_sems.at[2], ctx_size - 1)
    mq_out[...] = mq_back[...]
    settle(kv_back, recv_sems.at[3], ctx_size - 1)
    kv_out[...] = kv_back[...]
    settle(sum_in, recv_sems.at[5], ctx_size - 1)
    basis_out[...] = sum_in[...]

    settle(raw_in, send_sems.at[0], ctx_size - 1)
    settle(part_in, send_sems.at[1], ctx_size - 1)
    settle(mq_back, send_sems.at[2], ctx_size - 1)
    settle(kv_back, send_sems.at[3], ctx_size - 1)
    settle(half_buf, send_sems.at[4], tp_size - 1)
    settle(sum_in, send_sems.at[5], ctx_size - 1)


def unpack_kernel(
    dims,
    mq_ref,
    kv_ref,
    proj_ref,
    basis_ref,
    mixed_out,
    query_out,
    key_out,
    value_out,
    proj_out,
    basis_out,
):
    ctx_size, chans, folds, share = dims
    feat = ctx_size * share
    group = max(1, 16 // chans)
    for source, index, target in (
        (mq_ref, 0, mixed_out),
        (mq_ref, 1, query_out),
        (kv_ref, 0, key_out),
        (kv_ref, 1, value_out),
    ):
        for first in range(0, ctx_size, group):
            pieces = [source[first + other, index].astype(F32) for other in range(group)]
            for fold in range(folds):
                target[
                    first * chans : (first + group) * chans, fold * LANES : (fold + 1) * LANES
                ] = jnp.concatenate(
                    [piece[fold * chans : (fold + 1) * chans] for piece in pieces], axis=0
                ).astype(BF16)
    proj = jnp.concatenate([proj_ref[source] for source in range(ctx_size)], axis=0)
    proj_out[...] = jnp.transpose(proj)[:feat]
    basis = jnp.concatenate([basis_ref[source] for source in range(ctx_size)], axis=0)
    basis_out[...] = jnp.transpose(basis)[: basis_out.shape[0]]


def on_device(
    tables,
    query_in,
    key_in,
    value_in,
    short_kernel,
    basis_weight,
    basis_bias,
    filter_proj,
    decay_rate,
    skip_gain,
    grad_out,
):
    ctx_size = lax.axis_size("ctx")
    tp_size = lax.axis_size("tp")
    chan_local, num_tok = query_in.shape
    seq_total = num_tok * ctx_size
    chans = chan_local // ctx_size
    taps = short_kernel.shape[2]
    feat, emb = basis_weight.shape
    folds = num_tok // LANES
    slab = folds * chans
    blocks = seq_total // LANES
    rows = blocks * chans

    share = feat // ctx_size
    raw_slabs = (ctx_size, 4, slab, LANES)
    slabs = (ctx_size, 2, slab, LANES)
    dims = (ctx_size, tp_size, chans, seq_total, taps, feat, emb, chan_local * tp_size)
    vmem = pl.BlockSpec(memory_space=pltpu.VMEM)
    anywhere = pl.BlockSpec(memory_space=pl.ANY)
    landed = pl.pallas_call(
        functools.partial(mixer_kernel, dims),
        out_shape=(
            jax.ShapeDtypeStruct(slabs, BF16),
            jax.ShapeDtypeStruct(slabs, BF16),
            jax.ShapeDtypeStruct((ctx_size, chans, LANES), F32),
            jax.ShapeDtypeStruct((ctx_size, share, LANES), F32),
        ),
        in_specs=[vmem] * 10 + [anywhere] * len(tables),
        out_specs=(vmem, vmem, vmem, vmem),
        scratch_shapes=[pltpu.VMEM(table.shape, table.dtype) for table in tables]
        + [
            pltpu.VMEM(raw_slabs, BF16),
            pltpu.VMEM((LANES, chan_local), F32),
            pltpu.VMEM((chan_local, LANES), F32),
            pltpu.VMEM((BAND, LANES), F32),
            pltpu.VMEM(raw_slabs, BF16),
            pltpu.VMEM(slabs, BF16),
            pltpu.VMEM(slabs, BF16),
            pltpu.VMEM(slabs, BF16),
            pltpu.VMEM(slabs, BF16),
            pltpu.VMEM((2 * feat, seq_total), BF16),
            pltpu.VMEM((feat, seq_total), F32),
            pltpu.VMEM((rows, LANES), F32),
            pltpu.VMEM((rows, LANES), F32),
            pltpu.VMEM((ctx_size, chans + share, LANES), F32),
            pltpu.VMEM((ctx_size, chans + share, LANES), F32),
            pltpu.VMEM((tp_size, share, LANES), F32),
            pltpu.VMEM((share, LANES), F32),
            pltpu.VMEM((ctx_size, share, LANES), F32),
            pltpu.SemaphoreType.DMA((6,)),
            pltpu.SemaphoreType.DMA((6,)),
            pltpu.SemaphoreType.DMA((len(tables),)),
        ],
        compiler_params=pltpu.CompilerParams(
            collective_id=0, has_side_effects=True, vmem_limit_bytes=56 * 1024 * 1024
        ),
    )(
        query_in,
        key_in,
        value_in,
        grad_out,
        short_kernel.transpose(0, 2, 1),
        basis_weight.T,
        basis_bias[None, :],
        filter_proj.T,
        decay_rate[None, :],
        skip_gain[None, :],
        *tables,
    )
    block = jax.ShapeDtypeStruct((chan_local, num_tok), BF16)
    mixed, grad_query, grad_key, grad_value, proj_turned, basis_turned = pl.pallas_call(
        functools.partial(unpack_kernel, (ctx_size, chans, folds, share)),
        out_shape=(
            block,
            block,
            block,
            block,
            jax.ShapeDtypeStruct((feat, chan_local), F32),
            jax.ShapeDtypeStruct((emb, feat), F32),
        ),
        in_specs=[vmem] * 4,
        out_specs=(vmem,) * 6,
    )(*landed)
    return (mixed, grad_query, grad_key, grad_value, proj_turned.T, basis_turned.T)


def solution(mesh):
    ctx_size = mesh.shape["ctx"]

    def whole(*args):
        chans = args[0].shape[0] // mesh.shape["tp"] // ctx_size
        num_freq = (args[4].shape[1] - 1) // 2
        tables = constant_tables(args[0].shape[1], chans, num_freq)
        tables = tuple(jnp.asarray(table) for table in tables)
        return jax.shard_map(
            on_device,
            mesh=mesh,
            in_specs=(
                (P(),) * len(tables),
                P("tp", "ctx"),
                P("tp", "ctx"),
                P("tp", "ctx"),
                P(None, "tp", None),
                P(),
                P(),
                P("tp", None),
                P("tp"),
                P("tp"),
                P("tp", "ctx"),
            ),
            out_specs=(
                P("tp", "ctx"),
                P("tp", "ctx"),
                P("tp", "ctx"),
                P("tp", "ctx"),
                P("tp", None),
                P(),
            ),
            check_vma=False,
        )(tables, *args)

    return whole
```

```python
import functools
import math

import jax
import jax.numpy as jnp
import ml_dtypes
import numpy as np
from jax import lax
from jax.experimental import pallas as pl
from jax.experimental.pallas import tpu as pltpu
from jax.sharding import PartitionSpec as P

MESH = pl.DeviceIdType.MESH
BF16 = jnp.bfloat16
F32 = jnp.float32
LANES = 128
BAND = 40


def halves(table):
    high = table.astype(ml_dtypes.bfloat16)
    low = (table - high.astype(np.float64)).astype(ml_dtypes.bfloat16)
    return high, low


def constant_tables(seq_total, chans, num_freq):
    blocks = seq_total // LANES
    kept = blocks + 1
    period = 2 * blocks
    spec_rows = -(-kept * chans // 8) * 8
    eye = np.eye(chans)
    k1 = np.arange(kept)
    n1 = np.arange(blocks)
    n2 = np.arange(LANES)
    turn = 2.0 * np.pi * ((k1[:, None] * n1[None, :]) % period) / period
    fwd = np.zeros((2, spec_rows, blocks * chans))
    fwd[0, : kept * chans] = np.kron(np.cos(turn), eye)
    fwd[1, : kept * chans] = np.kron(-np.sin(turn), eye)
    weight = np.where((k1 == 0) | (k1 == blocks), 1.0, 2.0)[:, None] / (2.0 * seq_total)
    back = np.zeros((2, spec_rows, blocks * chans))
    back[0, : kept * chans] = np.kron(weight * np.cos(turn), eye)
    back[1, : kept * chans] = np.kron(-weight * np.sin(turn), eye)
    back = back.reshape(2 * spec_rows, blocks * chans)
    fwd = fwd.reshape(2 * spec_rows, blocks * chans)
    if chans % 8 == 0:
        used = np.r_[0:spec_rows, spec_rows + chans : 2 * spec_rows - chans]
        back = back[used]
        fwd = fwd[used]
    back = back.T.copy()
    twist = 2.0 * np.pi * ((k1[:, None] * n2[None, :]) % (2 * seq_total)) / (2 * seq_total)
    twiddle = np.zeros((2, spec_rows, LANES))
    twiddle[0, : kept * chans] = np.repeat(np.cos(twist), chans, axis=0)
    twiddle[1, : kept * chans] = np.repeat(-np.sin(twist), chans, axis=0)
    small = 2.0 * np.pi * ((n2[:, None] * n2[None, :]) % LANES) / LANES
    cos, sin = np.cos(small), np.sin(small)
    inner = np.block([[cos, -sin], [sin, cos]])
    inner_back = np.block([[cos, sin], [-sin, cos]])
    positions = np.arange(seq_total)
    basis = np.zeros((BAND, seq_total))
    basis[0] = positions / seq_total
    for harmonic in range(1, num_freq + 1):
        angles = 2.0 * np.pi * ((harmonic * positions) % seq_total) / seq_total
        basis[2 * harmonic - 1] = np.cos(angles)
        basis[2 * harmonic] = np.sin(angles)
    basis[2 * num_freq + 1] = 1.0
    first = basis.astype(ml_dtypes.bfloat16)
    rest = basis - first.astype(np.float64)
    second = rest.astype(ml_dtypes.bfloat16)
    third = (rest - second.astype(np.float64)).astype(ml_dtypes.bfloat16)
    rim = np.zeros((16, seq_total), ml_dtypes.bfloat16)
    basis_table = np.concatenate([first, second, third, first, second, first, rim])
    gap = np.zeros((LANES - 2 * BAND, seq_total), ml_dtypes.bfloat16)
    return (
        basis_table,
        np.concatenate([first, second, gap]).T.copy(),
        *halves(fwd),
        back.astype(ml_dtypes.bfloat16),
        inner.astype(ml_dtypes.bfloat16),
        inner_back.astype(ml_dtypes.bfloat16),
        twiddle.astype(np.float32),
    )


def dot(left, right):
    return jnp.dot(left, right, preferred_element_type=F32)


def dot_lanes(left, right):
    return lax.dot_general(left, right, (((1,), (1,)), ((), ())), preferred_element_type=F32)


def split(value):
    high = value.astype(BF16)
    return high, (value - high.astype(F32)).astype(BF16)


def sine_cosine(angle):
    quarter = jnp.floor(angle * (2.0 / math.pi) + 0.5)
    rest = angle - quarter * 1.5703125
    rest = rest - quarter * 4.837512969970703125e-4
    rest = rest - quarter * 7.54978995489188216e-8
    square = rest * rest
    sine = rest + rest * square * (
        -1.6666654611e-1 + square * (8.3321608736e-3 + square * -1.9515295891e-4)
    )
    cosine = (
        1.0
        - 0.5 * square
        + square
        * square
        * (4.166664568298827e-2 + square * (-1.388731625493765e-3 + square * 2.443315711809948e-5))
    )
    turns = quarter.astype(jnp.int32)
    odd = (turns & 1) == 1
    sin_out = jnp.where(odd, cosine, sine)
    cos_out = jnp.where(odd, sine, cosine)
    sin_out = jnp.where((turns & 2) == 2, -sin_out, sin_out)
    cos_out = jnp.where(((turns + 1) & 2) == 2, -cos_out, cos_out)
    return sin_out, cos_out


def mixer_kernel(
    dims,
    query_ref,
    key_ref,
    value_ref,
    grad_ref,
    taps_ref,
    weight_ref,
    bias_ref,
    proj_ref,
    decay_ref,
    skip_ref,
    basis_hbm,
    turned_hbm,
    fwd_hi_hbm,
    fwd_lo_hbm,
    back_hbm,
    inner_hbm,
    inv_hbm,
    twiddle_hbm,
    mq_out,
    kv_out,
    proj_out,
    basis_out,
    basis_ref,
    turned_ref,
    fwd_hi,
    fwd_lo,
    back_ref,
    inner_ref,
    inv_ref,
    twiddle_ref,
    raw_ref,
    par_buf,
    turn_buf,
    wide_buf,
    raw_in,
    mq_send,
    kv_send,
    mq_back,
    kv_back,
    act_buf,
    cos_buf,
    filt_buf,
    rows_buf,
    part_buf,
    part_in,
    half_buf,
    sum_buf,
    sum_in,
    send_sems,
    recv_sems,
    table_sems,
):
    ctx_size, tp_size, chans, seq_total, taps, feat, emb, tp_chans = dims
    me = lax.axis_index("ctx")
    my_tp = lax.axis_index("tp")
    blocks = seq_total // LANES
    rows = blocks * chans
    spec_rows = twiddle_ref.shape[1]
    slab = raw_ref.shape[2]
    chunk = 512

    def around(axis_size, own, body):
        def step(offset, carry):
            other = own + offset
            body(jnp.where(other >= axis_size, other - axis_size, other))
            return carry

        if axis_size <= 16:
            for offset in range(1, axis_size):
                step(offset, 0)
        else:
            lax.fori_loop(1, axis_size, step, 0)

    def others(body):
        around(ctx_size, me, body)

    def tp_others(body):
        around(tp_size, my_tp, body)

    barrier = pltpu.get_barrier_semaphore()

    def greet(ctx, tp):
        pl.semaphore_signal(
            barrier, inc=1, device_id={"ctx": ctx, "tp": tp}, device_id_type=MESH
        )

    others(lambda peer: greet(peer, my_tp))
    tp_others(lambda peer: greet(me, peer))

    loads = [
        pltpu.make_async_copy(source, target, table_sems.at[index])
        for index, (source, target) in enumerate(
            [
                (basis_hbm, basis_ref),
                (fwd_hi_hbm, fwd_hi),
                (fwd_lo_hbm, fwd_lo),
                (inner_hbm, inner_ref),
                (twiddle_hbm, twiddle_ref),
                (inv_hbm, inv_ref),
                (back_hbm, back_ref),
                (turned_hbm, turned_ref),
            ]
        )
    ]
    for load in loads:
        load.start()

    def pack(source, target, index):
        wide = source[...].astype(F32)
        for other in range(ctx_size):
            target[other, index] = jnp.concatenate(
                [
                    wide[other * chans : (other + 1) * chans, fold * LANES : (fold + 1) * LANES]
                    for fold in range(slab // chans)
                ],
                axis=0,
            ).astype(BF16)

    pack(key_ref, raw_ref, 0)
    pack(value_ref, raw_ref, 1)
    pack(query_ref, raw_ref, 2)
    pack(grad_ref, raw_ref, 3)
    pl.semaphore_wait(barrier, ctx_size + tp_size - 2)

    def push(src, dst, lane, ctx, tp):
        pltpu.make_async_remote_copy(
            src_ref=src,
            dst_ref=dst,
            send_sem=send_sems.at[lane],
            recv_sem=recv_sems.at[lane],
            device_id={"ctx": ctx, "tp": tp},
            device_id_type=MESH,
        ).start()

    def settle(ref, sem, count):
        part = ref.at[pl.ds(0, count)]
        pltpu.make_async_copy(part, part, sem).wait()

    others(lambda peer: push(raw_ref.at[peer], raw_in.at[me], 0, peer, my_tp))
    raw_in[me] = raw_ref[me]

    def expm1(value):
        series = 1.0 + value * (1.0 / 12.0)
        for order in range(11, 1, -1):
            series = 1.0 + value * series * (1.0 / order)
        return jnp.where(value > -0.5, value * series, jnp.exp(value) - 1.0)

    rates = decay_ref[...]
    energy = expm1(-2.0 * rates) / expm1(-2.0 * rates / seq_total)
    after = feat + 3 * taps
    par_buf[...] = jnp.zeros_like(par_buf)
    par_buf[0:feat] = proj_ref[...]
    for which in range(3):
        par_buf[feat + which * taps : feat + (which + 1) * taps] = taps_ref[which]
    par_buf[after : after + 1] = rates
    par_buf[after + 1 : after + 2] = 1.0 / jnp.sqrt(energy)
    par_buf[after + 2 : after + 3] = skip_ref[...]
    turn_buf[...] = jnp.transpose(par_buf[...])
    params = turn_buf[pl.ds(pl.multiple_of(me * chans, chans), chans), :]
    if chans < 8:
        params = jnp.concatenate([params] * (8 // chans), axis=0)

    def column(index):
        wide = jnp.broadcast_to(params[:, index : index + 1], (8, LANES))
        return jnp.concatenate([wide] * (rows // 8), axis=0)

    tap_at = feat
    decay = column(after)
    inv_energy = column(after + 1)
    skip = column(after + 2)

    lane_ids = lax.broadcasted_iota(jnp.int32, (rows, LANES), 1)
    row_ids = lax.broadcasted_iota(jnp.int32, (rows, LANES), 0)
    positions = ((row_ids // chans) * LANES + lane_ids).astype(F32)
    envelope = jnp.exp(-(decay * positions) / seq_total) * inv_energy

    wide_buf[...] = jnp.zeros_like(wide_buf)
    wide_buf[0:emb, 0:feat] = weight_ref[...]
    wide_buf[emb : emb + 1, 0:feat] = bias_ref[...]
    weight = jnp.concatenate([wide_buf[...]] * 6 + [jnp.zeros((16, LANES), F32)], axis=0)
    weight = jnp.transpose(weight)[0:feat]
    w_one = weight.astype(BF16)
    w_rest = weight - w_one.astype(F32)
    w_two = w_rest.astype(BF16)
    w_three = (w_rest - w_two.astype(F32)).astype(BF16)
    place = lax.broadcasted_iota(jnp.int32, weight.shape, 1)
    w_stack = jnp.where(
        place < 3 * BAND,
        w_one.astype(F32),
        jnp.where(place < 5 * BAND, w_two.astype(F32), w_three.astype(F32)),
    ).astype(BF16)

    own_proj = params[:, :feat]
    proj_hi, proj_lo = split(own_proj)
    proj_hi = proj_hi.astype(F32)
    proj_lo = proj_lo.astype(F32)
    proj_stack = jnp.concatenate(
        [
            jnp.concatenate([proj_hi, proj_hi], axis=1),
            jnp.concatenate([proj_lo, proj_lo], axis=1),
        ],
        axis=0,
    ).astype(BF16)

    def activate(here):
        hidden = dot(w_stack, basis_ref[:, here])
        act, cosine = sine_cosine(hidden)
        cos_buf[:, here] = cosine
        act_hi, act_lo = split(act)
        act_buf[0:feat, here] = act_hi
        act_buf[feat : 2 * feat, here] = act_lo

    def filter_step(index, carry):
        here = pl.ds(pl.multiple_of(index * chunk, chunk), chunk)
        activate(here)
        both = dot(proj_stack, act_buf[:, here])
        piece = both[0:8] + both[8:16]
        for block in range(chunk // LANES):
            at = pl.multiple_of((index * (chunk // LANES) + block) * chans, chans)
            filt_buf[pl.ds(at, chans), :] = piece[
                0:chans, block * LANES : (block + 1) * LANES
            ]
        return carry

    loads[0].wait()
    if chans % 8 == 0:
        for index in range(seq_total // chunk):
            activate(pl.ds(index * chunk, chunk))
        both = dot(proj_stack, act_buf[...])
        piece = both[0:8] + both[8:16]
        filt = jnp.concatenate(
            [piece[:, block * LANES : (block + 1) * LANES] for block in range(blocks)], axis=0
        )
    else:
        lax.fori_loop(0, seq_total // chunk, filter_step, 0)
        filt = filt_buf[...]
    filt = (filt * envelope).astype(BF16)

    blank = jnp.zeros((chans, LANES), F32)

    def spectra(signals):
        count = len(signals)
        both = jnp.concatenate(signals, axis=1) if count > 1 else signals[0]
        outer = dot(fwd_hi[...], both) + dot(fwd_lo[...], both)
        tw_re, tw_im = twiddle_ref[0], twiddle_ref[1]
        turned = []
        for index in range(count):
            own = outer[:, index * LANES : (index + 1) * LANES]
            out_re, out_im = own[:spec_rows], own[spec_rows:]
            if chans % 8 == 0:
                out_im = jnp.concatenate([blank, out_im, blank], axis=0)
            turned.append(
                jnp.concatenate(
                    [out_re * tw_re - out_im * tw_im, out_re * tw_im + out_im * tw_re], axis=1
                )
            )
        high, low = split(jnp.concatenate(turned, axis=0) if count > 1 else turned[0])
        spec = dot(high, inner_ref[...]) + dot(low, inner_ref[...])
        return [
            (
                spec[index * spec_rows : (index + 1) * spec_rows, :LANES],
                spec[index * spec_rows : (index + 1) * spec_rows, LANES:],
            )
            for index in range(count)
        ]

    def restore(spec_re, spec_im):
        high, low = split(jnp.concatenate([spec_re, spec_im], axis=1))
        section = dot(high, inv_ref[...]) + dot(low, inv_ref[...])
        sec_re, sec_im = section[:, :LANES], section[:, LANES:]
        tw_re, tw_im = twiddle_ref[0], twiddle_ref[1]
        turn_im = sec_im * tw_re - sec_re * tw_im
        if chans % 8 == 0:
            turn_im = turn_im[chans : spec_rows - chans]
        turned = jnp.concatenate([sec_re * tw_re + sec_im * tw_im, turn_im], axis=0)
        high, low = split(turned)
        pair = dot(back_ref[...], jnp.concatenate([high, low], axis=1))
        return pair[:, :LANES] + pair[:, LANES:]

    def to_rows(ref, index):
        if slab % 16 == 0:
            return ref[:, index].reshape(rows, LANES).astype(F32)
        for source in range(ctx_size):
            rows_buf[source * slab : (source + 1) * slab, :] = ref[source, index].astype(F32)
        return rows_buf[...]

    def from_rows(ref, index, value):
        if slab % 16 == 0:
            ref[:, index] = value.reshape(ctx_size, slab, LANES)
        else:
            rows_buf[...] = value.astype(F32)
            for target in range(ctx_size):
                ref[target, index] = rows_buf[target * slab : (target + 1) * slab, :].astype(BF16)

    def down(value):
        if chans % 8 == 0:
            return jnp.concatenate([blank, value[: rows - chans]], axis=0)
        return jnp.where(row_ids < chans, 0.0, pltpu.roll(value, chans, 0))

    def up(value):
        if chans % 8 == 0:
            return jnp.concatenate([value[chans:], blank], axis=0)
        return jnp.where(row_ids >= rows - chans, 0.0, pltpu.roll(value, rows - chans, 0))

    def featurize(signal, which):
        result = column(tap_at + which * taps) * signal
        for offset in range(1, taps):
            turned = pltpu.roll(signal, offset, 1)
            shifted = jnp.where(lane_ids < offset, down(turned), turned)
            result = result + column(tap_at + which * taps + offset) * shifted
        return result

    def featurize_back(signal, which):
        result = column(tap_at + which * taps) * signal
        for offset in range(1, taps):
            turned = pltpu.roll(signal, LANES - offset, 1)
            shifted = jnp.where(lane_ids >= LANES - offset, up(turned), turned)
            result = result + column(tap_at + which * taps + offset) * shifted
        return result

    for load in loads[1:]:
        load.wait()
    ((filt_re, filt_im),) = spectra([filt])

    settle(raw_in, recv_sems.at[0], ctx_size - 1)
    key_feat = featurize(to_rows(raw_in, 0), 1)
    value_feat = featurize(to_rows(raw_in, 1), 2)
    query_feat = featurize(to_rows(raw_in, 2), 0)
    grad_wide = to_rows(raw_in, 3)
    carried = (key_feat * value_feat).astype(BF16)
    grad_long = (grad_wide * query_feat).astype(BF16)
    (carried_re, carried_im), (grad_re, grad_im) = spectra([carried, grad_long])

    long_out = restore(
        filt_re * carried_re - filt_im * carried_im, filt_re * carried_im + filt_im * carried_re
    )
    long_out = (long_out + skip * carried.astype(F32)).astype(BF16).astype(F32)

    from_rows(mq_send, 0, (query_feat * long_out).astype(BF16))
    grad_query_feat = (grad_wide * long_out).astype(BF16).astype(F32)
    from_rows(mq_send, 1, featurize_back(grad_query_feat, 0).astype(BF16))
    others(lambda peer: push(mq_send.at[peer], mq_back.at[me], 2, peer, my_tp))

    filter_grad = restore(
        carried_re * grad_re + carried_im * grad_im, carried_re * grad_im - carried_im * grad_re
    )
    grad_raw = filter_grad.astype(BF16).astype(F32) * envelope
    if chans % 8 == 0:
        raw_wide = jnp.concatenate(
            [grad_raw[block * chans : (block + 1) * chans] for block in range(blocks)], axis=1
        )
    else:
        rows_buf[...] = grad_raw
        raw_wide = jnp.concatenate(
            [
                jnp.concatenate(
                    [
                        rows_buf[block * chans : (block + 1) * chans, :],
                        jnp.zeros((8 - chans, LANES), F32),
                    ],
                    axis=0,
                )
                for block in range(blocks)
            ],
            axis=1,
        )
    raw_hi, raw_lo = split(raw_wide)
    raw_hi = raw_hi.astype(F32)
    raw_lo = raw_lo.astype(F32)
    raw_two = jnp.concatenate([raw_hi, raw_lo], axis=0).astype(BF16)
    gp_all = jnp.transpose(dot_lanes(act_buf[...], raw_two))
    gp_all = gp_all[0:8] + gp_all[8:16]
    gp = gp_all + pltpu.roll(gp_all, feat, 1)
    gp = gp[0:chans] * (1.0 / math.sqrt(seq_total))

    turned_params = jnp.transpose(params)[:feat]
    pt_hi, pt_lo = split(turned_params)
    pt_hi = pt_hi.astype(F32)
    pt_lo = pt_lo.astype(F32)
    pt_stack = jnp.concatenate([pt_hi, pt_lo, pt_hi, pt_lo], axis=1).astype(BF16)
    raw_four = jnp.concatenate([raw_hi, raw_hi, raw_lo, raw_lo], axis=0).astype(BF16)
    grad_hidden = dot(pt_stack, raw_four) * cos_buf[...]
    gh_hi, gh_lo = split(grad_hidden)
    gh_stack = jnp.concatenate([gh_hi, gh_lo], axis=0)
    gb_all = dot(gh_stack, turned_ref[...])
    gb_all = gb_all[:feat] + gb_all[feat:]
    gb = (gb_all + pltpu.roll(gb_all, LANES - BAND, 1)) * math.sqrt(
        feat / (seq_total * tp_chans)
    )
    share = feat // ctx_size
    for target in range(ctx_size):
        part_buf[target, 0:chans] = gp
        part_buf[target, chans : chans + share] = gb[target * share : (target + 1) * share]
    others(lambda peer: push(part_buf.at[peer], part_in.at[me], 1, peer, my_tp))
    part_in[me] = part_buf[me]

    carried_grad = restore(
        filt_re * grad_re + filt_im * grad_im, filt_re * grad_im - filt_im * grad_re
    )
    carried_grad = (carried_grad + skip * grad_long.astype(F32)).astype(BF16).astype(F32)
    grad_key_feat = (carried_grad * value_feat).astype(BF16).astype(F32)
    grad_value_feat = (carried_grad * key_feat).astype(BF16).astype(F32)
    from_rows(kv_send, 0, featurize_back(grad_key_feat, 1).astype(BF16))
    from_rows(kv_send, 1, featurize_back(grad_value_feat, 2).astype(BF16))
    settle(part_in, recv_sems.at[1], ctx_size - 1)
    half_buf[my_tp] = jnp.sum(part_in[:, chans : chans + share], axis=0)
    tp_others(lambda peer: push(half_buf.at[my_tp], half_buf.at[my_tp], 4, me, peer))
    others(lambda peer: push(kv_send.at[peer], kv_back.at[me], 3, peer, my_tp))

    settle(half_buf, recv_sems.at[4], tp_size - 1)
    sum_buf[...] = jnp.sum(half_buf[...], axis=0)
    others(lambda peer: push(sum_buf, sum_in.at[me], 5, peer, my_tp))
    sum_in[me] = sum_buf[...]
    mq_back[me] = mq_send[me]
    kv_back[me] = kv_send[me]
    proj_out[...] = part_in[:, 0:chans]
    settle(mq_back, recv_sems.at[2], ctx_size - 1)
    mq_out[...] = mq_back[...]
    settle(kv_back, recv_sems.at[3], ctx_size - 1)
    kv_out[...] = kv_back[...]
    settle(sum_in, recv_sems.at[5], ctx_size - 1)
    basis_out[...] = sum_in[...]

    settle(raw_in, send_sems.at[0], ctx_size - 1)
    settle(part_in, send_sems.at[1], ctx_size - 1)
    settle(mq_back, send_sems.at[2], ctx_size - 1)
    settle(kv_back, send_sems.at[3], ctx_size - 1)
    settle(half_buf, send_sems.at[4], tp_size - 1)
    settle(sum_in, send_sems.at[5], ctx_size - 1)


def unpack_kernel(
    dims,
    mq_ref,
    kv_ref,
    proj_ref,
    basis_ref,
    mixed_out,
    query_out,
    key_out,
    value_out,
    proj_out,
    basis_out,
):
    ctx_size, chans, folds, share = dims
    feat = ctx_size * share
    group = max(1, 16 // chans)
    for source, index, target in (
        (mq_ref, 0, mixed_out),
        (mq_ref, 1, query_out),
        (kv_ref, 0, key_out),
        (kv_ref, 1, value_out),
    ):
        for first in range(0, ctx_size, group):
            pieces = [source[first + other, index].astype(F32) for other in range(group)]
            for fold in range(folds):
                target[
                    first * chans : (first + group) * chans, fold * LANES : (fold + 1) * LANES
                ] = jnp.concatenate(
                    [piece[fold * chans : (fold + 1) * chans] for piece in pieces], axis=0
                ).astype(BF16)
    proj = jnp.concatenate([proj_ref[source] for source in range(ctx_size)], axis=0)
    proj_out[...] = jnp.transpose(proj)[:feat]
    basis = jnp.concatenate([basis_ref[source] for source in range(ctx_size)], axis=0)
    basis_out[...] = jnp.transpose(basis)[: basis_out.shape[0]]


def on_device(
    tables,
    query_in,
    key_in,
    value_in,
    short_kernel,
    basis_weight,
    basis_bias,
    filter_proj,
    decay_rate,
    skip_gain,
    grad_out,
):
    ctx_size = lax.axis_size("ctx")
    tp_size = lax.axis_size("tp")
    chan_local, num_tok = query_in.shape
    seq_total = num_tok * ctx_size
    chans = chan_local // ctx_size
    taps = short_kernel.shape[2]
    feat, emb = basis_weight.shape
    folds = num_tok // LANES
    slab = folds * chans
    blocks = seq_total // LANES
    rows = blocks * chans

    share = feat // ctx_size
    raw_slabs = (ctx_size, 4, slab, LANES)
    slabs = (ctx_size, 2, slab, LANES)
    dims = (ctx_size, tp_size, chans, seq_total, taps, feat, emb, chan_local * tp_size)
    vmem = pl.BlockSpec(memory_space=pltpu.VMEM)
    anywhere = pl.BlockSpec(memory_space=pl.ANY)
    landed = pl.pallas_call(
        functools.partial(mixer_kernel, dims),
        out_shape=(
            jax.ShapeDtypeStruct(slabs, BF16),
            jax.ShapeDtypeStruct(slabs, BF16),
            jax.ShapeDtypeStruct((ctx_size, chans, LANES), F32),
            jax.ShapeDtypeStruct((ctx_size, share, LANES), F32),
        ),
        in_specs=[vmem] * 10 + [anywhere] * len(tables),
        out_specs=(vmem, vmem, vmem, vmem),
        scratch_shapes=[pltpu.VMEM(table.shape, table.dtype) for table in tables]
        + [
            pltpu.VMEM(raw_slabs, BF16),
            pltpu.VMEM((LANES, chan_local), F32),
            pltpu.VMEM((chan_local, LANES), F32),
            pltpu.VMEM((BAND, LANES), F32),
            pltpu.VMEM(raw_slabs, BF16),
            pltpu.VMEM(slabs, BF16),
            pltpu.VMEM(slabs, BF16),
            pltpu.VMEM(slabs, BF16),
            pltpu.VMEM(slabs, BF16),
            pltpu.VMEM((2 * feat, seq_total), BF16),
            pltpu.VMEM((feat, seq_total), F32),
            pltpu.VMEM((rows, LANES), F32),
            pltpu.VMEM((rows, LANES), F32),
            pltpu.VMEM((ctx_size, chans + share, LANES), F32),
            pltpu.VMEM((ctx_size, chans + share, LANES), F32),
            pltpu.VMEM((tp_size, share, LANES), F32),
            pltpu.VMEM((share, LANES), F32),
            pltpu.VMEM((ctx_size, share, LANES), F32),
            pltpu.SemaphoreType.DMA((6,)),
            pltpu.SemaphoreType.DMA((6,)),
            pltpu.SemaphoreType.DMA((len(tables),)),
        ],
        compiler_params=pltpu.CompilerParams(
            collective_id=0, has_side_effects=True, vmem_limit_bytes=56 * 1024 * 1024
        ),
    )(
        query_in,
        key_in,
        value_in,
        grad_out,
        short_kernel.transpose(0, 2, 1),
        basis_weight.T,
        basis_bias[None, :],
        filter_proj.T,
        decay_rate[None, :],
        skip_gain[None, :],
        *tables,
    )
    block = jax.ShapeDtypeStruct((chan_local, num_tok), BF16)
    mixed, grad_query, grad_key, grad_value, proj_turned, basis_turned = pl.pallas_call(
        functools.partial(unpack_kernel, (ctx_size, chans, folds, share)),
        out_shape=(
            block,
            block,
            block,
            block,
            jax.ShapeDtypeStruct((feat, chan_local), F32),
            jax.ShapeDtypeStruct((emb, feat), F32),
        ),
        in_specs=[vmem] * 4,
        out_specs=(vmem,) * 6,
    )(*landed)
    return (mixed, grad_query, grad_key, grad_value, proj_turned.T, basis_turned.T)


def solution(mesh):
    ctx_size = mesh.shape["ctx"]

    def whole(*args):
        chans = args[0].shape[0] // mesh.shape["tp"] // ctx_size
        num_freq = (args[4].shape[1] - 1) // 2
        tables = constant_tables(args[0].shape[1], chans, num_freq)
        tables = tuple(jnp.asarray(table) for table in tables)
        return jax.shard_map(
            on_device,
            mesh=mesh,
            in_specs=(
                (P(),) * len(tables),
                P("tp", "ctx"),
                P("tp", "ctx"),
                P("tp", "ctx"),
                P(None, "tp", None),
                P(),
                P(),
                P("tp", None),
                P("tp"),
                P("tp"),
                P("tp", "ctx"),
            ),
            out_specs=(
                P("tp", "ctx"),
                P("tp", "ctx"),
                P("tp", "ctx"),
                P("tp", "ctx"),
                P("tp", None),
                P(),
            ),
            check_vma=False,
        )(tables, *args)

    return whole
```

```python
import functools
import math

import jax
import jax.numpy as jnp
import ml_dtypes
import numpy as np
from jax import lax
from jax.experimental import pallas as pl
from jax.experimental.pallas import tpu as pltpu
from jax.sharding import PartitionSpec as P

MESH = pl.DeviceIdType.MESH
BF16 = jnp.bfloat16
F32 = jnp.float32
LANES = 128
BAND = 40


def halves(table):
    high = table.astype(ml_dtypes.bfloat16)
    low = (table - high.astype(np.float64)).astype(ml_dtypes.bfloat16)
    return high, low


def constant_tables(seq_total, chans, num_freq):
    blocks = seq_total // LANES
    kept = blocks + 1
    period = 2 * blocks
    spec_rows = -(-kept * chans // 8) * 8
    eye = np.eye(chans)
    k1 = np.arange(kept)
    n1 = np.arange(blocks)
    n2 = np.arange(LANES)
    turn = 2.0 * np.pi * ((k1[:, None] * n1[None, :]) % period) / period
    fwd = np.zeros((2, spec_rows, blocks * chans))
    fwd[0, : kept * chans] = np.kron(np.cos(turn), eye)
    fwd[1, : kept * chans] = np.kron(-np.sin(turn), eye)
    weight = np.where((k1 == 0) | (k1 == blocks), 1.0, 2.0)[:, None] / (2.0 * seq_total)
    back = np.zeros((2, spec_rows, blocks * chans))
    back[0, : kept * chans] = np.kron(weight * np.cos(turn), eye)
    back[1, : kept * chans] = np.kron(-weight * np.sin(turn), eye)
    back = back.reshape(2 * spec_rows, blocks * chans)
    fwd = fwd.reshape(2 * spec_rows, blocks * chans)
    if chans % 8 == 0:
        used = np.r_[0:spec_rows, spec_rows + chans : 2 * spec_rows - chans]
        back = back[used]
        fwd = fwd[used]
    back = back.T.copy()
    twist = 2.0 * np.pi * ((k1[:, None] * n2[None, :]) % (2 * seq_total)) / (2 * seq_total)
    twiddle = np.zeros((2, spec_rows, LANES))
    twiddle[0, : kept * chans] = np.repeat(np.cos(twist), chans, axis=0)
    twiddle[1, : kept * chans] = np.repeat(-np.sin(twist), chans, axis=0)
    small = 2.0 * np.pi * ((n2[:, None] * n2[None, :]) % LANES) / LANES
    cos, sin = np.cos(small), np.sin(small)
    inner = np.block([[cos, -sin], [sin, cos]])
    inner_back = np.block([[cos, sin], [-sin, cos]])
    positions = np.arange(seq_total)
    basis = np.zeros((BAND, seq_total))
    basis[0] = positions / seq_total
    for harmonic in range(1, num_freq + 1):
        angles = 2.0 * np.pi * ((harmonic * positions) % seq_total) / seq_total
        basis[2 * harmonic - 1] = np.cos(angles)
        basis[2 * harmonic] = np.sin(angles)
    basis[2 * num_freq + 1] = 1.0
    first = basis.astype(ml_dtypes.bfloat16)
    rest = basis - first.astype(np.float64)
    second = rest.astype(ml_dtypes.bfloat16)
    third = (rest - second.astype(np.float64)).astype(ml_dtypes.bfloat16)
    rim = np.zeros((16, seq_total), ml_dtypes.bfloat16)
    basis_table = np.concatenate([first, second, third, first, second, first, rim])
    gap = np.zeros((LANES - 2 * BAND, seq_total), ml_dtypes.bfloat16)
    return (
        basis_table,
        np.concatenate([first, second, gap]).T.copy(),
        *halves(fwd),
        *halves(back),
        *halves(inner),
        *halves(inner_back),
        twiddle.astype(np.float32),
    )


def dot(left, right):
    return jnp.dot(left, right, preferred_element_type=F32)


def dot_lanes(left, right):
    return lax.dot_general(left, right, (((1,), (1,)), ((), ())), preferred_element_type=F32)


def split(value):
    high = value.astype(BF16)
    return high, (value - high.astype(F32)).astype(BF16)


def sine_cosine(angle):
    quarter = jnp.floor(angle * (2.0 / math.pi) + 0.5)
    rest = angle - quarter * 1.5703125
    rest = rest - quarter * 4.837512969970703125e-4
    rest = rest - quarter * 7.54978995489188216e-8
    square = rest * rest
    sine = rest + rest * square * (
        -1.6666654611e-1 + square * (8.3321608736e-3 + square * -1.9515295891e-4)
    )
    cosine = (
        1.0
        - 0.5 * square
        + square
        * square
        * (4.166664568298827e-2 + square * (-1.388731625493765e-3 + square * 2.443315711809948e-5))
    )
    turns = quarter.astype(jnp.int32)
    odd = (turns & 1) == 1
    sin_out = jnp.where(odd, cosine, sine)
    cos_out = jnp.where(odd, sine, cosine)
    sin_out = jnp.where((turns & 2) == 2, -sin_out, sin_out)
    cos_out = jnp.where(((turns + 1) & 2) == 2, -cos_out, cos_out)
    return sin_out, cos_out


def mixer_kernel(
    dims,
    query_ref,
    key_ref,
    value_ref,
    grad_ref,
    taps_ref,
    weight_ref,
    bias_ref,
    proj_ref,
    decay_ref,
    skip_ref,
    basis_hbm,
    turned_hbm,
    fwd_hi_hbm,
    fwd_lo_hbm,
    back_hi_hbm,
    back_lo_hbm,
    inner_hi_hbm,
    inner_lo_hbm,
    inv_hi_hbm,
    inv_lo_hbm,
    twiddle_hbm,
    mixed_out,
    query_out,
    key_out,
    value_out,
    proj_out,
    basis_out,
    basis_ref,
    turned_ref,
    fwd_hi,
    fwd_lo,
    back_hi,
    back_lo,
    inner_hi,
    inner_lo,
    inv_hi,
    inv_lo,
    twiddle_ref,
    raw_ref,
    par_buf,
    turn_buf,
    wide_buf,
    raw_in,
    long_send,
    back_send,
    long_back,
    back_in,
    rim_send,
    rim_in,
    end_send,
    end_in,
    query_buf,
    key_buf,
    value_buf,
    act_buf,
    cos_buf,
    filt_buf,
    rows_buf,
    part_buf,
    part_in,
    half_buf,
    sum_buf,
    sum_in,
    send_sems,
    recv_sems,
    table_sems,
):
    ctx_size, tp_size, chans, seq_total, taps, feat, emb, tp_chans = dims
    me = lax.axis_index("ctx")
    my_tp = lax.axis_index("tp")
    blocks = seq_total // LANES
    rows = blocks * chans
    spec_rows = twiddle_ref.shape[1]
    slab = raw_ref.shape[2]
    chunk = 512

    def around(axis_size, own, body):
        def step(offset, carry):
            other = own + offset
            body(jnp.where(other >= axis_size, other - axis_size, other))
            return carry

        if axis_size <= 16:
            for offset in range(1, axis_size):
                step(offset, 0)
        else:
            lax.fori_loop(1, axis_size, step, 0)

    def others(body):
        around(ctx_size, me, body)

    def tp_others(body):
        around(tp_size, my_tp, body)

    barrier = pltpu.get_barrier_semaphore()

    def greet(ctx, tp):
        pl.semaphore_signal(
            barrier, inc=1, device_id={"ctx": ctx, "tp": tp}, device_id_type=MESH
        )

    others(lambda peer: greet(peer, my_tp))
    tp_others(lambda peer: greet(me, peer))

    loads = [
        pltpu.make_async_copy(source, target, table_sems.at[index])
        for index, (source, target) in enumerate(
            [
                (basis_hbm, basis_ref),
                (fwd_hi_hbm, fwd_hi),
                (fwd_lo_hbm, fwd_lo),
                (inner_hi_hbm, inner_hi),
                (inner_lo_hbm, inner_lo),
                (twiddle_hbm, twiddle_ref),
                (inv_hi_hbm, inv_hi),
                (inv_lo_hbm, inv_lo),
                (back_hi_hbm, back_hi),
                (back_lo_hbm, back_lo),
                (turned_hbm, turned_ref),
            ]
        )
    ]
    for load in loads:
        load.start()

    def push(src, dst, lane, ctx, tp):
        pltpu.make_async_remote_copy(
            src_ref=src,
            dst_ref=dst,
            send_sem=send_sems.at[lane],
            recv_sem=recv_sems.at[lane],
            device_id={"ctx": ctx, "tp": tp},
            device_id_type=MESH,
        ).start()

    def settle(ref, sem, count):
        part = ref.at[pl.ds(0, count)]
        pltpu.make_async_copy(part, part, sem).wait()

    def expm1(value):
        series = 1.0 + value * (1.0 / 12.0)
        for order in range(11, 1, -1):
            series = 1.0 + value * series * (1.0 / order)
        return jnp.where(value > -0.5, value * series, jnp.exp(value) - 1.0)

    rates = decay_ref[...]
    energy = expm1(-2.0 * rates) / expm1(-2.0 * rates / seq_total)
    after = feat + 3 * taps
    par_buf[...] = jnp.zeros_like(par_buf)
    par_buf[0:feat] = proj_ref[...]
    for which in range(3):
        par_buf[feat + which * taps : feat + (which + 1) * taps] = taps_ref[which]
    par_buf[after : after + 1] = rates
    par_buf[after + 1 : after + 2] = 1.0 / jnp.sqrt(energy)
    par_buf[after + 2 : after + 3] = skip_ref[...]
    turn_buf[...] = jnp.transpose(par_buf[...])
    params = turn_buf[pl.ds(pl.multiple_of(me * chans, chans), chans), :]
    if chans < 8:
        params = jnp.concatenate([params] * (8 // chans), axis=0)

    folds = slab // chans
    tile_lanes = lax.broadcasted_iota(jnp.int32, (proj_ref.shape[1], LANES), 1)
    next_ctx = jnp.where(me == ctx_size - 1, 0, me + 1)
    prev_ctx = jnp.where(me == 0, ctx_size - 1, me - 1)

    def tiles(ref):
        wide = ref[...].astype(F32)
        return [wide[:, fold * LANES : (fold + 1) * LANES] for fold in range(folds)]

    def put(ref, parts):
        for fold in range(folds):
            ref[:, fold * LANES : (fold + 1) * LANES] = parts[fold].astype(ref.dtype)

    def tap(which, offset):
        at = feat + which * taps + offset
        return jnp.broadcast_to(turn_buf[:, at : at + 1], tile_lanes.shape)

    query, key, value = tiles(query_ref), tiles(key_ref), tiles(value_ref)
    rim_send[...] = jnp.where(
        tile_lanes >= LANES - 16,
        query[-1],
        jnp.where(
            tile_lanes >= LANES - 32,
            pltpu.roll(key[-1], LANES - 16, 1),
            pltpu.roll(value[-1], LANES - 32, 1),
        ),
    ).astype(BF16)
    pl.semaphore_wait(barrier, ctx_size + tp_size - 2)
    push(rim_send, rim_in, 0, next_ctx, my_tp)

    def column(index):
        wide = jnp.broadcast_to(params[:, index : index + 1], (8, LANES))
        return jnp.concatenate([wide] * (rows // 8), axis=0)

    decay = column(after)
    inv_energy = column(after + 1)
    skip = column(after + 2)

    lane_ids = lax.broadcasted_iota(jnp.int32, (rows, LANES), 1)
    row_ids = lax.broadcasted_iota(jnp.int32, (rows, LANES), 0)
    positions = ((row_ids // chans) * LANES + lane_ids).astype(F32)
    envelope = jnp.exp(-(decay * positions) / seq_total) * inv_energy

    wide_buf[...] = jnp.zeros_like(wide_buf)
    wide_buf[0:emb, 0:feat] = weight_ref[...]
    wide_buf[emb : emb + 1, 0:feat] = bias_ref[...]
    weight = jnp.concatenate([wide_buf[...]] * 6 + [jnp.zeros((16, LANES), F32)], axis=0)
    weight = jnp.transpose(weight)[0:feat]
    w_one = weight.astype(BF16)
    w_rest = weight - w_one.astype(F32)
    w_two = w_rest.astype(BF16)
    w_three = (w_rest - w_two.astype(F32)).astype(BF16)
    place = lax.broadcasted_iota(jnp.int32, weight.shape, 1)
    w_stack = jnp.where(
        place < 3 * BAND,
        w_one.astype(F32),
        jnp.where(place < 5 * BAND, w_two.astype(F32), w_three.astype(F32)),
    ).astype(BF16)

    own_proj = params[:, :feat]
    proj_hi, proj_lo = split(own_proj)
    proj_hi = proj_hi.astype(F32)
    proj_lo = proj_lo.astype(F32)
    proj_stack = jnp.concatenate(
        [
            jnp.concatenate([proj_hi, proj_hi], axis=1),
            jnp.concatenate([proj_lo, proj_lo], axis=1),
        ],
        axis=0,
    ).astype(BF16)

    def activate(here):
        hidden = dot(w_stack, basis_ref[:, here])
        act, cosine = sine_cosine(hidden)
        cos_buf[:, here] = cosine
        act_hi, act_lo = split(act)
        act_buf[0:feat, here] = act_hi
        act_buf[feat : 2 * feat, here] = act_lo

    def filter_step(index, carry):
        here = pl.ds(pl.multiple_of(index * chunk, chunk), chunk)
        activate(here)
        both = dot(proj_stack, act_buf[:, here])
        piece = both[0:8] + both[8:16]
        for block in range(chunk // LANES):
            at = pl.multiple_of((index * (chunk // LANES) + block) * chans, chans)
            filt_buf[pl.ds(at, chans), :] = piece[
                0:chans, block * LANES : (block + 1) * LANES
            ]
        return carry

    loads[0].wait()
    steps = seq_total // chunk
    if chans % 8 == 0:
        for index in range(steps // 2):
            activate(pl.ds(index * chunk, chunk))

    pltpu.make_async_copy(rim_in, rim_in, recv_sems.at[0]).wait()
    rim = jnp.where(me == 0, 0.0, rim_in[...].astype(F32))

    def featurize(parts, before, which):
        result = [tap(which, 0) * part for part in parts]
        for offset in range(1, taps):
            turned = [pltpu.roll(part, offset, 1) for part in [before, *parts]]
            weight_here = tap(which, offset)
            for fold in range(folds):
                shifted = jnp.where(tile_lanes < offset, turned[fold], turned[fold + 1])
                result[fold] = result[fold] + weight_here * shifted
        return result

    def pack(parts, index):
        for other in range(ctx_size):
            raw_ref[other, index] = jnp.concatenate(
                [part[other * chans : (other + 1) * chans] for part in parts], axis=0
            ).astype(BF16)

    query_feat = featurize(query, rim, 0)
    key_feat = featurize(key, pltpu.roll(rim, 16, 1), 1)
    value_feat = featurize(value, pltpu.roll(rim, 32, 1), 2)
    put(query_buf, query_feat)
    put(key_buf, key_feat)
    put(value_buf, value_feat)
    pack([left * right for left, right in zip(key_feat, value_feat)], 0)
    pack([left * right for left, right in zip(query_feat, tiles(grad_ref))], 1)
    others(lambda peer: push(raw_ref.at[peer], raw_in.at[me], 3, peer, my_tp))
    raw_in[me] = raw_ref[me]

    if chans % 8 == 0:
        for index in range(steps // 2, steps):
            activate(pl.ds(index * chunk, chunk))
        both = dot(proj_stack, act_buf[...])
        piece = both[0:8] + both[8:16]
        filt = jnp.concatenate(
            [piece[:, block * LANES : (block + 1) * LANES] for block in range(blocks)], axis=0
        )
    else:
        lax.fori_loop(0, steps, filter_step, 0)
        filt = filt_buf[...]
    filt = (filt * envelope).astype(BF16)

    blank = jnp.zeros((chans, LANES), F32)

    def spectra(signals):
        count = len(signals)
        both = jnp.concatenate(signals, axis=1) if count > 1 else signals[0]
        outer = dot(fwd_hi[...], both) + dot(fwd_lo[...], both)
        tw_re, tw_im = twiddle_ref[0], twiddle_ref[1]
        turned = []
        for index in range(count):
            own = outer[:, index * LANES : (index + 1) * LANES]
            out_re, out_im = own[:spec_rows], own[spec_rows:]
            if chans % 8 == 0:
                out_im = jnp.concatenate([blank, out_im, blank], axis=0)
            turned.append(
                jnp.concatenate(
                    [out_re * tw_re - out_im * tw_im, out_re * tw_im + out_im * tw_re], axis=1
                )
            )
        high, low = split(jnp.concatenate(turned, axis=0) if count > 1 else turned[0])
        spec = dot(high, inner_hi[...]) + dot(high, inner_lo[...]) + dot(low, inner_hi[...])
        return [
            (
                spec[index * spec_rows : (index + 1) * spec_rows, :LANES],
                spec[index * spec_rows : (index + 1) * spec_rows, LANES:],
            )
            for index in range(count)
        ]

    def restore(spec_re, spec_im):
        high, low = split(jnp.concatenate([spec_re, spec_im], axis=1))
        section = dot(high, inv_hi[...]) + dot(high, inv_lo[...]) + dot(low, inv_hi[...])
        sec_re, sec_im = section[:, :LANES], section[:, LANES:]
        tw_re, tw_im = twiddle_ref[0], twiddle_ref[1]
        turn_im = sec_im * tw_re - sec_re * tw_im
        if chans % 8 == 0:
            turn_im = turn_im[chans : spec_rows - chans]
        turned = jnp.concatenate([sec_re * tw_re + sec_im * tw_im, turn_im], axis=0)
        high, low = split(turned)
        pair = dot(back_hi[...], jnp.concatenate([high, low], axis=1))
        return pair[:, :LANES] + pair[:, LANES:] + dot(back_lo[...], high)

    def to_rows(ref, index):
        if slab % 16 == 0:
            return ref[:, index].reshape(rows, LANES).astype(F32)
        for source in range(ctx_size):
            rows_buf[source * slab : (source + 1) * slab, :] = ref[source, index].astype(F32)
        return rows_buf[...]

    def from_rows(ref, value):
        if slab % 16 == 0:
            ref[...] = value.reshape(ctx_size, slab, LANES)
        else:
            rows_buf[...] = value.astype(F32)
            for target in range(ctx_size):
                ref[target] = rows_buf[target * slab : (target + 1) * slab, :].astype(BF16)

    def to_tiles(ref):
        pieces = [ref[source].astype(F32) for source in range(ctx_size)]
        return [
            jnp.concatenate(
                [piece[fold * chans : (fold + 1) * chans] for piece in pieces], axis=0
            )
            for fold in range(folds)
        ]

    def featurize_back(parts, after_it, which):
        result = [tap(which, 0) * part for part in parts]
        for offset in range(1, taps):
            turned = [pltpu.roll(part, LANES - offset, 1) for part in [*parts, after_it]]
            weight_here = tap(which, offset)
            for fold in range(folds):
                shifted = jnp.where(
                    tile_lanes >= LANES - offset, turned[fold + 1], turned[fold]
                )
                result[fold] = result[fold] + weight_here * shifted
        return result

    for load in loads[1:]:
        load.wait()
    ((filt_re, filt_im),) = spectra([filt])

    settle(raw_in, recv_sems.at[3], ctx_size - 1)
    carried = to_rows(raw_in, 0).astype(BF16)
    grad_long = to_rows(raw_in, 1).astype(BF16)
    (carried_re, carried_im), (grad_re, grad_im) = spectra([carried, grad_long])

    long_out = restore(
        filt_re * carried_re - filt_im * carried_im, filt_re * carried_im + filt_im * carried_re
    )
    from_rows(long_send, (long_out + skip * carried.astype(F32)).astype(BF16))
    others(lambda peer: push(long_send.at[peer], long_back.at[me], 2, peer, my_tp))
    long_back[me] = long_send[me]

    filter_grad = restore(
        carried_re * grad_re + carried_im * grad_im, carried_re * grad_im - carried_im * grad_re
    )
    grad_raw = filter_grad.astype(BF16).astype(F32) * envelope
    if chans % 8 == 0:
        raw_wide = jnp.concatenate(
            [grad_raw[block * chans : (block + 1) * chans] for block in range(blocks)], axis=1
        )
    else:
        rows_buf[...] = grad_raw
        raw_wide = jnp.concatenate(
            [
                jnp.concatenate(
                    [
                        rows_buf[block * chans : (block + 1) * chans, :],
                        jnp.zeros((8 - chans, LANES), F32),
                    ],
                    axis=0,
                )
                for block in range(blocks)
            ],
            axis=1,
        )
    raw_hi, raw_lo = split(raw_wide)
    raw_hi = raw_hi.astype(F32)
    raw_lo = raw_lo.astype(F32)
    raw_two = jnp.concatenate([raw_hi, raw_lo], axis=0).astype(BF16)
    gp_all = jnp.transpose(dot_lanes(act_buf[...], raw_two))
    gp_all = gp_all[0:8] + gp_all[8:16]
    gp = gp_all + pltpu.roll(gp_all, feat, 1)
    gp = gp[0:chans] * (1.0 / math.sqrt(seq_total))

    turned_params = jnp.transpose(params)[:feat]
    pt_hi, pt_lo = split(turned_params)
    pt_hi = pt_hi.astype(F32)
    pt_lo = pt_lo.astype(F32)
    pt_stack = jnp.concatenate([pt_hi, pt_lo, pt_hi, pt_lo], axis=1).astype(BF16)
    raw_four = jnp.concatenate([raw_hi, raw_hi, raw_lo, raw_lo], axis=0).astype(BF16)
    grad_hidden = dot(pt_stack, raw_four) * cos_buf[...]
    gh_hi, gh_lo = split(grad_hidden)
    gh_stack = jnp.concatenate([gh_hi, gh_lo], axis=0)
    gb_all = dot(gh_stack, turned_ref[...])
    gb_all = gb_all[:feat] + gb_all[feat:]
    gb = (gb_all + pltpu.roll(gb_all, LANES - BAND, 1)) * math.sqrt(
        feat / (seq_total * tp_chans)
    )
    share = feat // ctx_size
    for target in range(ctx_size):
        part_buf[target, 0:chans] = gp
        part_buf[target, chans : chans + share] = gb[target * share : (target + 1) * share]
    others(lambda peer: push(part_buf.at[peer], part_in.at[me], 1, peer, my_tp))
    part_in[me] = part_buf[me]

    carried_grad = restore(
        filt_re * grad_re + filt_im * grad_im, filt_re * grad_im - filt_im * grad_re
    )
    from_rows(back_send, (carried_grad + skip * grad_long.astype(F32)).astype(BF16))
    others(lambda peer: push(back_send.at[peer], back_in.at[me], 6, peer, my_tp))
    back_in[me] = back_send[me]
    settle(part_in, recv_sems.at[1], ctx_size - 1)
    half_buf[my_tp] = jnp.sum(part_in[:, chans : chans + share], axis=0)
    tp_others(lambda peer: push(half_buf.at[my_tp], half_buf.at[my_tp], 4, me, peer))

    settle(long_back, recv_sems.at[2], ctx_size - 1)
    long_tok = to_tiles(long_back)
    put(mixed_out, [left * right for left, right in zip(tiles(query_buf), long_tok)])

    def rounded(left, right):
        return [(one * two).astype(BF16).astype(F32) for one, two in zip(left, right)]

    grad_query_feat = rounded(tiles(grad_ref), long_tok)

    settle(half_buf, recv_sems.at[4], tp_size - 1)
    sum_buf[...] = jnp.sum(half_buf[...], axis=0)
    others(lambda peer: push(sum_buf, sum_in.at[me], 5, peer, my_tp))
    sum_in[me] = sum_buf[...]

    settle(back_in, recv_sems.at[6], ctx_size - 1)
    carried_tok = to_tiles(back_in)
    grad_key_feat = rounded(carried_tok, tiles(value_buf))
    grad_value_feat = rounded(carried_tok, tiles(key_buf))
    end_send[...] = jnp.where(
        tile_lanes < 16,
        grad_query_feat[0],
        jnp.where(
            tile_lanes < 32,
            pltpu.roll(grad_key_feat[0], 16, 1),
            pltpu.roll(grad_value_feat[0], 32, 1),
        ),
    ).astype(BF16)
    push(end_send, end_in, 7, prev_ctx, my_tp)
    proj = jnp.concatenate([part_in[source, 0:chans] for source in range(ctx_size)], axis=0)
    proj_out[...] = jnp.transpose(proj)[:feat]
    settle(sum_in, recv_sems.at[5], ctx_size - 1)
    basis = jnp.concatenate([sum_in[source] for source in range(ctx_size)], axis=0)
    basis_out[...] = jnp.transpose(basis)[:emb]

    pltpu.make_async_copy(end_in, end_in, recv_sems.at[7]).wait()
    end = jnp.where(me == ctx_size - 1, 0.0, end_in[...].astype(F32))
    put(query_out, featurize_back(grad_query_feat, end, 0))
    put(key_out, featurize_back(grad_key_feat, pltpu.roll(end, LANES - 16, 1), 1))
    put(value_out, featurize_back(grad_value_feat, pltpu.roll(end, LANES - 32, 1), 2))

    pltpu.make_async_copy(rim_in, rim_in, send_sems.at[0]).wait()
    settle(part_in, send_sems.at[1], ctx_size - 1)
    settle(long_back, send_sems.at[2], ctx_size - 1)
    settle(raw_in, send_sems.at[3], ctx_size - 1)
    settle(half_buf, send_sems.at[4], tp_size - 1)
    settle(sum_in, send_sems.at[5], ctx_size - 1)
    settle(back_in, send_sems.at[6], ctx_size - 1)
    pltpu.make_async_copy(end_in, end_in, send_sems.at[7]).wait()


def on_device(
    tables,
    query_in,
    key_in,
    value_in,
    short_kernel,
    basis_weight,
    basis_bias,
    filter_proj,
    decay_rate,
    skip_gain,
    grad_out,
):
    ctx_size = lax.axis_size("ctx")
    tp_size = lax.axis_size("tp")
    chan_local, num_tok = query_in.shape
    seq_total = num_tok * ctx_size
    chans = chan_local // ctx_size
    taps = short_kernel.shape[2]
    feat, emb = basis_weight.shape
    folds = num_tok // LANES
    slab = folds * chans
    blocks = seq_total // LANES
    rows = blocks * chans

    share = feat // ctx_size
    raw_slabs = (ctx_size, 2, slab, LANES)
    slabs = (ctx_size, slab, LANES)
    dims = (ctx_size, tp_size, chans, seq_total, taps, feat, emb, chan_local * tp_size)
    vmem = pl.BlockSpec(memory_space=pltpu.VMEM)
    anywhere = pl.BlockSpec(memory_space=pl.ANY)
    block = jax.ShapeDtypeStruct((chan_local, num_tok), BF16)
    mixed, grad_query, grad_key, grad_value, proj_turned, basis_turned = pl.pallas_call(
        functools.partial(mixer_kernel, dims),
        out_shape=(
            block,
            block,
            block,
            block,
            jax.ShapeDtypeStruct((feat, chan_local), F32),
            jax.ShapeDtypeStruct((emb, feat), F32),
        ),
        in_specs=[vmem] * 10 + [anywhere] * len(tables),
        out_specs=(vmem,) * 6,
        scratch_shapes=[pltpu.VMEM(table.shape, table.dtype) for table in tables]
        + [
            pltpu.VMEM(raw_slabs, BF16),
            pltpu.VMEM((LANES, chan_local), F32),
            pltpu.VMEM((chan_local, LANES), F32),
            pltpu.VMEM((BAND, LANES), F32),
            pltpu.VMEM(raw_slabs, BF16),
            pltpu.VMEM(slabs, BF16),
            pltpu.VMEM(slabs, BF16),
            pltpu.VMEM(slabs, BF16),
            pltpu.VMEM(slabs, BF16),
            pltpu.VMEM((chan_local, LANES), BF16),
            pltpu.VMEM((chan_local, LANES), BF16),
            pltpu.VMEM((chan_local, LANES), BF16),
            pltpu.VMEM((chan_local, LANES), BF16),
            pltpu.VMEM((chan_local, num_tok), F32),
            pltpu.VMEM((chan_local, num_tok), F32),
            pltpu.VMEM((chan_local, num_tok), F32),
            pltpu.VMEM((2 * feat, seq_total), BF16),
            pltpu.VMEM((feat, seq_total), F32),
            pltpu.VMEM((rows, LANES), F32),
            pltpu.VMEM((rows, LANES), F32),
            pltpu.VMEM((ctx_size, chans + share, LANES), F32),
            pltpu.VMEM((ctx_size, chans + share, LANES), F32),
            pltpu.VMEM((tp_size, share, LANES), F32),
            pltpu.VMEM((share, LANES), F32),
            pltpu.VMEM((ctx_size, share, LANES), F32),
            pltpu.SemaphoreType.DMA((8,)),
            pltpu.SemaphoreType.DMA((8,)),
            pltpu.SemaphoreType.DMA((len(tables),)),
        ],
        compiler_params=pltpu.CompilerParams(
            collective_id=0, has_side_effects=True, vmem_limit_bytes=56 * 1024 * 1024
        ),
    )(
        query_in,
        key_in,
        value_in,
        grad_out,
        short_kernel.transpose(0, 2, 1),
        basis_weight.T,
        basis_bias[None, :],
        filter_proj.T,
        decay_rate[None, :],
        skip_gain[None, :],
        *tables,
    )
    return (mixed, grad_query, grad_key, grad_value, proj_turned.T, basis_turned.T)


def solution(mesh):
    ctx_size = mesh.shape["ctx"]

    def whole(*args):
        chans = args[0].shape[0] // mesh.shape["tp"] // ctx_size
        num_freq = (args[4].shape[1] - 1) // 2
        tables = constant_tables(args[0].shape[1], chans, num_freq)
        tables = tuple(jnp.asarray(table) for table in tables)
        return jax.shard_map(
            on_device,
            mesh=mesh,
            in_specs=(
                (P(),) * len(tables),
                P("tp", "ctx"),
                P("tp", "ctx"),
                P("tp", "ctx"),
                P(None, "tp", None),
                P(),
                P(),
                P("tp", None),
                P("tp"),
                P("tp"),
                P("tp", "ctx"),
            ),
            out_specs=(
                P("tp", "ctx"),
                P("tp", "ctx"),
                P("tp", "ctx"),
                P("tp", "ctx"),
                P("tp", None),
                P(),
            ),
            check_vma=False,
        )(tables, *args)

    return whole
```

```python
import functools
import math

import jax
import jax.numpy as jnp
import ml_dtypes
import numpy as np
from jax import lax
from jax.experimental import pallas as pl
from jax.experimental.pallas import tpu as pltpu
from jax.sharding import PartitionSpec as P

MESH = pl.DeviceIdType.MESH
BF16 = jnp.bfloat16
F32 = jnp.float32
LANES = 128
BAND = 40


def halves(table):
    high = table.astype(ml_dtypes.bfloat16)
    low = (table - high.astype(np.float64)).astype(ml_dtypes.bfloat16)
    return high, low


def constant_tables(seq_total, chans, num_freq):
    blocks = seq_total // LANES
    kept = blocks + 1
    period = 2 * blocks
    spec_rows = -(-kept * chans // 8) * 8
    eye = np.eye(chans)
    k1 = np.arange(kept)
    n1 = np.arange(blocks)
    n2 = np.arange(LANES)
    turn = 2.0 * np.pi * ((k1[:, None] * n1[None, :]) % period) / period
    fwd = np.zeros((2, spec_rows, blocks * chans))
    fwd[0, : kept * chans] = np.kron(np.cos(turn), eye)
    fwd[1, : kept * chans] = np.kron(-np.sin(turn), eye)
    weight = np.where((k1 == 0) | (k1 == blocks), 1.0, 2.0)[:, None] / (2.0 * seq_total)
    back = np.zeros((2, spec_rows, blocks * chans))
    back[0, : kept * chans] = np.kron(weight * np.cos(turn), eye)
    back[1, : kept * chans] = np.kron(-weight * np.sin(turn), eye)
    back = back.reshape(2 * spec_rows, blocks * chans)
    fwd = fwd.reshape(2 * spec_rows, blocks * chans)
    if chans % 8 == 0:
        used = np.r_[0:spec_rows, spec_rows + chans : 2 * spec_rows - chans]
        back = back[used]
        fwd = fwd[used]
    back = back.T.copy()
    twist = 2.0 * np.pi * ((k1[:, None] * n2[None, :]) % (2 * seq_total)) / (2 * seq_total)
    twiddle = np.zeros((2, spec_rows, LANES))
    twiddle[0, : kept * chans] = np.repeat(np.cos(twist), chans, axis=0)
    twiddle[1, : kept * chans] = np.repeat(-np.sin(twist), chans, axis=0)
    small = 2.0 * np.pi * ((n2[:, None] * n2[None, :]) % LANES) / LANES
    cos, sin = np.cos(small), np.sin(small)
    inner = np.block([[cos, -sin], [sin, cos]])
    inner_back = np.block([[cos, sin], [-sin, cos]])
    positions = np.arange(seq_total)
    basis = np.zeros((BAND, seq_total))
    basis[0] = positions / seq_total
    for harmonic in range(1, num_freq + 1):
        angles = 2.0 * np.pi * ((harmonic * positions) % seq_total) / seq_total
        basis[2 * harmonic - 1] = np.cos(angles)
        basis[2 * harmonic] = np.sin(angles)
    basis[2 * num_freq + 1] = 1.0
    first = basis.astype(ml_dtypes.bfloat16)
    rest = basis - first.astype(np.float64)
    second = rest.astype(ml_dtypes.bfloat16)
    third = (rest - second.astype(np.float64)).astype(ml_dtypes.bfloat16)
    rim = np.zeros((16, seq_total), ml_dtypes.bfloat16)
    basis_table = np.concatenate([first, second, third, first, second, first, rim])
    gap = np.zeros((LANES - 2 * BAND, seq_total), ml_dtypes.bfloat16)
    return (
        basis_table,
        np.concatenate([first, second, gap]).T.copy(),
        *halves(fwd),
        back.astype(ml_dtypes.bfloat16),
        inner.astype(ml_dtypes.bfloat16),
        inner_back.astype(ml_dtypes.bfloat16),
        twiddle.astype(np.float32),
    )


def dot(left, right):
    return jnp.dot(left, right, preferred_element_type=F32)


def dot_lanes(left, right):
    return lax.dot_general(left, right, (((1,), (1,)), ((), ())), preferred_element_type=F32)


def split(value):
    high = value.astype(BF16)
    return high, (value - high.astype(F32)).astype(BF16)


def sine_cosine(angle):
    quarter = jnp.floor(angle * (2.0 / math.pi) + 0.5)
    rest = angle - quarter * 1.5703125
    rest = rest - quarter * 4.837512969970703125e-4
    rest = rest - quarter * 7.54978995489188216e-8
    square = rest * rest
    sine = rest + rest * square * (
        -1.6666654611e-1 + square * (8.3321608736e-3 + square * -1.9515295891e-4)
    )
    cosine = (
        1.0
        - 0.5 * square
        + square
        * square
        * (4.166664568298827e-2 + square * (-1.388731625493765e-3 + square * 2.443315711809948e-5))
    )
    turns = quarter.astype(jnp.int32)
    odd = (turns & 1) == 1
    sin_out = jnp.where(odd, cosine, sine)
    cos_out = jnp.where(odd, sine, cosine)
    sin_out = jnp.where((turns & 2) == 2, -sin_out, sin_out)
    cos_out = jnp.where(((turns + 1) & 2) == 2, -cos_out, cos_out)
    return sin_out, cos_out


def mixer_kernel(
    dims,
    query_ref,
    key_ref,
    value_ref,
    grad_ref,
    taps_ref,
    weight_ref,
    bias_ref,
    proj_ref,
    decay_ref,
    skip_ref,
    basis_hbm,
    turned_hbm,
    fwd_hi_hbm,
    fwd_lo_hbm,
    back_hbm,
    inner_hbm,
    inv_hbm,
    twiddle_hbm,
    mq_out,
    kv_out,
    proj_out,
    basis_out,
    basis_ref,
    turned_ref,
    fwd_hi,
    fwd_lo,
    back_ref,
    inner_ref,
    inv_ref,
    twiddle_ref,
    raw_ref,
    par_buf,
    turn_buf,
    wide_buf,
    raw_in,
    mq_send,
    kv_send,
    mq_back,
    kv_back,
    act_buf,
    cos_buf,
    filt_buf,
    rows_buf,
    part_buf,
    part_in,
    half_buf,
    sum_buf,
    sum_in,
    send_sems,
    recv_sems,
    table_sems,
):
    ctx_size, tp_size, chans, seq_total, taps, feat, emb, tp_chans = dims
    me = lax.axis_index("ctx")
    my_tp = lax.axis_index("tp")
    blocks = seq_total // LANES
    rows = blocks * chans
    spec_rows = twiddle_ref.shape[1]
    slab = raw_ref.shape[2]
    chunk = 512

    def around(axis_size, own, body):
        def step(offset, carry):
            other = own + offset
            body(jnp.where(other >= axis_size, other - axis_size, other))
            return carry

        if axis_size <= 2:
            for offset in range(1, axis_size):
                step(offset, 0)
        else:
            lax.fori_loop(1, axis_size, step, 0)

    def others(body):
        around(ctx_size, me, body)

    def tp_others(body):
        around(tp_size, my_tp, body)

    barrier = pltpu.get_barrier_semaphore()

    def greet(ctx, tp):
        pl.semaphore_signal(
            barrier, inc=1, device_id={"ctx": ctx, "tp": tp}, device_id_type=MESH
        )

    others(lambda peer: greet(peer, my_tp))
    tp_others(lambda peer: greet(me, peer))

    loads = [
        pltpu.make_async_copy(source, target, table_sems.at[index])
        for index, (source, target) in enumerate(
            [
                (basis_hbm, basis_ref),
                (fwd_hi_hbm, fwd_hi),
                (fwd_lo_hbm, fwd_lo),
                (inner_hbm, inner_ref),
                (twiddle_hbm, twiddle_ref),
                (inv_hbm, inv_ref),
                (back_hbm, back_ref),
                (turned_hbm, turned_ref),
            ]
        )
    ]
    for load in loads:
        load.start()

    def pack(source, target, index):
        wide = source[...].astype(F32)
        for other in range(ctx_size):
            target[other, index] = jnp.concatenate(
                [
                    wide[other * chans : (other + 1) * chans, fold * LANES : (fold + 1) * LANES]
                    for fold in range(slab // chans)
                ],
                axis=0,
            ).astype(BF16)

    pack(key_ref, raw_ref, 0)
    pack(value_ref, raw_ref, 1)
    pack(query_ref, raw_ref, 2)
    pack(grad_ref, raw_ref, 3)
    pl.semaphore_wait(barrier, ctx_size + tp_size - 2)

    def push(src, dst, lane, ctx, tp):
        pltpu.make_async_remote_copy(
            src_ref=src,
            dst_ref=dst,
            send_sem=send_sems.at[lane],
            recv_sem=recv_sems.at[lane],
            device_id={"ctx": ctx, "tp": tp},
            device_id_type=MESH,
        ).start()

    def settle(ref, sem, count):
        part = ref.at[pl.ds(0, count)]
        pltpu.make_async_copy(part, part, sem).wait()

    others(lambda peer: push(raw_ref.at[peer], raw_in.at[me], 0, peer, my_tp))
    raw_in[me] = raw_ref[me]

    def expm1(value):
        series = 1.0 + value * (1.0 / 12.0)
        for order in range(11, 1, -1):
            series = 1.0 + value * series * (1.0 / order)
        return jnp.where(value > -0.5, value * series, jnp.exp(value) - 1.0)

    rates = decay_ref[...]
    energy = expm1(-2.0 * rates) / expm1(-2.0 * rates / seq_total)
    after = feat + 3 * taps
    par_buf[...] = jnp.zeros_like(par_buf)
    par_buf[0:feat] = proj_ref[...]
    for which in range(3):
        par_buf[feat + which * taps : feat + (which + 1) * taps] = taps_ref[which]
    par_buf[after : after + 1] = rates
    par_buf[after + 1 : after + 2] = 1.0 / jnp.sqrt(energy)
    par_buf[after + 2 : after + 3] = skip_ref[...]
    turn_buf[...] = jnp.transpose(par_buf[...])
    params = turn_buf[pl.ds(pl.multiple_of(me * chans, chans), chans), :]
    if chans < 8:
        params = jnp.concatenate([params] * (8 // chans), axis=0)

    def column(index):
        wide = jnp.broadcast_to(params[:, index : index + 1], (8, LANES))
        return jnp.concatenate([wide] * (rows // 8), axis=0)

    tap_at = feat
    decay = column(after)
    inv_energy = column(after + 1)
    skip = column(after + 2)

    lane_ids = lax.broadcasted_iota(jnp.int32, (rows, LANES), 1)
    row_ids = lax.broadcasted_iota(jnp.int32, (rows, LANES), 0)
    positions = ((row_ids // chans) * LANES + lane_ids).astype(F32)
    envelope = jnp.exp(-(decay * positions) / seq_total) * inv_energy

    wide_buf[...] = jnp.zeros_like(wide_buf)
    wide_buf[0:emb, 0:feat] = weight_ref[...]
    wide_buf[emb : emb + 1, 0:feat] = bias_ref[...]
    weight = jnp.concatenate([wide_buf[...]] * 6 + [jnp.zeros((16, LANES), F32)], axis=0)
    weight = jnp.transpose(weight)[0:feat]
    w_one = weight.astype(BF16)
    w_rest = weight - w_one.astype(F32)
    w_two = w_rest.astype(BF16)
    w_three = (w_rest - w_two.astype(F32)).astype(BF16)
    place = lax.broadcasted_iota(jnp.int32, weight.shape, 1)
    w_stack = jnp.where(
        place < 3 * BAND,
        w_one.astype(F32),
        jnp.where(place < 5 * BAND, w_two.astype(F32), w_three.astype(F32)),
    ).astype(BF16)

    own_proj = params[:, :feat]
    proj_hi, proj_lo = split(own_proj)
    proj_hi = proj_hi.astype(F32)
    proj_lo = proj_lo.astype(F32)
    proj_stack = jnp.concatenate(
        [
            jnp.concatenate([proj_hi, proj_hi], axis=1),
            jnp.concatenate([proj_lo, proj_lo], axis=1),
        ],
        axis=0,
    ).astype(BF16)

    def activate(here):
        hidden = dot(w_stack, basis_ref[:, here])
        act, cosine = sine_cosine(hidden)
        cos_buf[:, here] = cosine
        act_hi, act_lo = split(act)
        act_buf[0:feat, here] = act_hi
        act_buf[feat : 2 * feat, here] = act_lo

    def filter_step(index, carry):
        here = pl.ds(pl.multiple_of(index * chunk, chunk), chunk)
        activate(here)
        both = dot(proj_stack, act_buf[:, here])
        piece = both[0:8] + both[8:16]
        for block in range(chunk // LANES):
            at = pl.multiple_of((index * (chunk // LANES) + block) * chans, chans)
            filt_buf[pl.ds(at, chans), :] = piece[
                0:chans, block * LANES : (block + 1) * LANES
            ]
        return carry

    loads[0].wait()
    if chans % 8 == 0:

        def activate_step(index, carry):
            activate(pl.ds(pl.multiple_of(index * chunk, chunk), chunk))
            return carry

        lax.fori_loop(0, seq_total // chunk, activate_step, 0)
        both = dot(proj_stack, act_buf[...])
        piece = both[0:8] + both[8:16]
        filt = jnp.concatenate(
            [piece[:, block * LANES : (block + 1) * LANES] for block in range(blocks)], axis=0
        )
    else:
        lax.fori_loop(0, seq_total // chunk, filter_step, 0)
        filt = filt_buf[...]
    filt = (filt * envelope).astype(BF16)

    blank = jnp.zeros((chans, LANES), F32)

    def spectra(signals):
        count = len(signals)
        both = jnp.concatenate(signals, axis=1) if count > 1 else signals[0]
        outer = dot(fwd_hi[...], both) + dot(fwd_lo[...], both)
        tw_re, tw_im = twiddle_ref[0], twiddle_ref[1]
        turned = []
        for index in range(count):
            own = outer[:, index * LANES : (index + 1) * LANES]
            out_re, out_im = own[:spec_rows], own[spec_rows:]
            if chans % 8 == 0:
                out_im = jnp.concatenate([blank, out_im, blank], axis=0)
            turned.append(
                jnp.concatenate(
                    [out_re * tw_re - out_im * tw_im, out_re * tw_im + out_im * tw_re], axis=1
                )
            )
        high, low = split(jnp.concatenate(turned, axis=0) if count > 1 else turned[0])
        spec = dot(high, inner_ref[...]) + dot(low, inner_ref[...])
        return [
            (
                spec[index * spec_rows : (index + 1) * spec_rows, :LANES],
                spec[index * spec_rows : (index + 1) * spec_rows, LANES:],
            )
            for index in range(count)
        ]

    def restore(spec_re, spec_im):
        high, low = split(jnp.concatenate([spec_re, spec_im], axis=1))
        section = dot(high, inv_ref[...]) + dot(low, inv_ref[...])
        sec_re, sec_im = section[:, :LANES], section[:, LANES:]
        tw_re, tw_im = twiddle_ref[0], twiddle_ref[1]
        turn_im = sec_im * tw_re - sec_re * tw_im
        if chans % 8 == 0:
            turn_im = turn_im[chans : spec_rows - chans]
        turned = jnp.concatenate([sec_re * tw_re + sec_im * tw_im, turn_im], axis=0)
        high, low = split(turned)
        pair = dot(back_ref[...], jnp.concatenate([high, low], axis=1))
        return pair[:, :LANES] + pair[:, LANES:]

    def to_rows(ref, index):
        if slab % 16 == 0:
            return ref[:, index].reshape(rows, LANES).astype(F32)
        for source in range(ctx_size):
            rows_buf[source * slab : (source + 1) * slab, :] = ref[source, index].astype(F32)
        return rows_buf[...]

    def from_rows(ref, index, value):
        if slab % 16 == 0:
            ref[:, index] = value.reshape(ctx_size, slab, LANES)
        else:
            rows_buf[...] = value.astype(F32)
            for target in range(ctx_size):
                ref[target, index] = rows_buf[target * slab : (target + 1) * slab, :].astype(BF16)

    def down(value):
        if chans % 8 == 0:
            return jnp.concatenate([blank, value[: rows - chans]], axis=0)
        return jnp.where(row_ids < chans, 0.0, pltpu.roll(value, chans, 0))

    def up(value):
        if chans % 8 == 0:
            return jnp.concatenate([value[chans:], blank], axis=0)
        return jnp.where(row_ids >= rows - chans, 0.0, pltpu.roll(value, rows - chans, 0))

    def featurize(signal, which):
        result = column(tap_at + which * taps) * signal
        for offset in range(1, taps):
            turned = pltpu.roll(signal, offset, 1)
            shifted = jnp.where(lane_ids < offset, down(turned), turned)
            result = result + column(tap_at + which * taps + offset) * shifted
        return result

    def featurize_back(signal, which):
        result = column(tap_at + which * taps) * signal
        for offset in range(1, taps):
            turned = pltpu.roll(signal, LANES - offset, 1)
            shifted = jnp.where(lane_ids >= LANES - offset, up(turned), turned)
            result = result + column(tap_at + which * taps + offset) * shifted
        return result

    for load in loads[1:]:
        load.wait()
    ((filt_re, filt_im),) = spectra([filt])

    settle(raw_in, recv_sems.at[0], ctx_size - 1)
    key_feat = featurize(to_rows(raw_in, 0), 1)
    value_feat = featurize(to_rows(raw_in, 1), 2)
    query_feat = featurize(to_rows(raw_in, 2), 0)
    grad_wide = to_rows(raw_in, 3)
    carried = (key_feat * value_feat).astype(BF16)
    grad_long = (grad_wide * query_feat).astype(BF16)
    (carried_re, carried_im), (grad_re, grad_im) = spectra([carried, grad_long])

    long_out = restore(
        filt_re * carried_re - filt_im * carried_im, filt_re * carried_im + filt_im * carried_re
    )
    long_out = (long_out + skip * carried.astype(F32)).astype(BF16).astype(F32)

    from_rows(mq_send, 0, (query_feat * long_out).astype(BF16))
    grad_query_feat = (grad_wide * long_out).astype(BF16).astype(F32)
    from_rows(mq_send, 1, featurize_back(grad_query_feat, 0).astype(BF16))
    others(lambda peer: push(mq_send.at[peer], mq_back.at[me], 2, peer, my_tp))

    filter_grad = restore(
        carried_re * grad_re + carried_im * grad_im, carried_re * grad_im - carried_im * grad_re
    )
    grad_raw = filter_grad.astype(BF16).astype(F32) * envelope
    if chans % 8 == 0:
        raw_wide = jnp.concatenate(
            [grad_raw[block * chans : (block + 1) * chans] for block in range(blocks)], axis=1
        )
    else:
        rows_buf[...] = grad_raw
        raw_wide = jnp.concatenate(
            [
                jnp.concatenate(
                    [
                        rows_buf[block * chans : (block + 1) * chans, :],
                        jnp.zeros((8 - chans, LANES), F32),
                    ],
                    axis=0,
                )
                for block in range(blocks)
            ],
            axis=1,
        )
    raw_hi, raw_lo = split(raw_wide)
    raw_hi = raw_hi.astype(F32)
    raw_lo = raw_lo.astype(F32)
    raw_two = jnp.concatenate([raw_hi, raw_lo], axis=0).astype(BF16)
    gp_all = jnp.transpose(dot_lanes(act_buf[...], raw_two))
    gp_all = gp_all[0:8] + gp_all[8:16]
    gp = gp_all + pltpu.roll(gp_all, feat, 1)
    gp = gp[0:chans] * (1.0 / math.sqrt(seq_total))

    turned_params = jnp.transpose(params)[:feat]
    pt_hi, pt_lo = split(turned_params)
    pt_hi = pt_hi.astype(F32)
    pt_lo = pt_lo.astype(F32)
    pt_stack = jnp.concatenate([pt_hi, pt_lo, pt_hi, pt_lo], axis=1).astype(BF16)
    raw_four = jnp.concatenate([raw_hi, raw_hi, raw_lo, raw_lo], axis=0).astype(BF16)
    grad_hidden = dot(pt_stack, raw_four) * cos_buf[...]
    gh_hi, gh_lo = split(grad_hidden)
    gh_stack = jnp.concatenate([gh_hi, gh_lo], axis=0)
    gb_all = dot(gh_stack, turned_ref[...])
    gb_all = gb_all[:feat] + gb_all[feat:]
    gb = (gb_all + pltpu.roll(gb_all, LANES - BAND, 1)) * math.sqrt(
        feat / (seq_total * tp_chans)
    )
    share = feat // ctx_size
    for target in range(ctx_size):
        part_buf[target, 0:chans] = gp
        part_buf[target, chans : chans + share] = gb[target * share : (target + 1) * share]
    others(lambda peer: push(part_buf.at[peer], part_in.at[me], 1, peer, my_tp))
    part_in[me] = part_buf[me]

    carried_grad = restore(
        filt_re * grad_re + filt_im * grad_im, filt_re * grad_im - filt_im * grad_re
    )
    carried_grad = (carried_grad + skip * grad_long.astype(F32)).astype(BF16).astype(F32)
    grad_key_feat = (carried_grad * value_feat).astype(BF16).astype(F32)
    grad_value_feat = (carried_grad * key_feat).astype(BF16).astype(F32)
    from_rows(kv_send, 0, featurize_back(grad_key_feat, 1).astype(BF16))
    from_rows(kv_send, 1, featurize_back(grad_value_feat, 2).astype(BF16))
    others(lambda peer: push(kv_send.at[peer], kv_back.at[me], 3, peer, my_tp))
    settle(part_in, recv_sems.at[1], ctx_size - 1)
    half_buf[my_tp] = jnp.sum(part_in[:, chans : chans + share], axis=0)
    tp_others(lambda peer: push(half_buf.at[my_tp], half_buf.at[my_tp], 4, me, peer))

    settle(half_buf, recv_sems.at[4], tp_size - 1)
    sum_buf[...] = jnp.sum(half_buf[...], axis=0)
    others(lambda peer: push(sum_buf, sum_in.at[me], 5, peer, my_tp))
    sum_in[me] = sum_buf[...]
    mq_back[me] = mq_send[me]
    kv_back[me] = kv_send[me]
    proj_out[...] = part_in[:, 0:chans]
    settle(mq_back, recv_sems.at[2], ctx_size - 1)
    mq_out[...] = mq_back[...]
    settle(kv_back, recv_sems.at[3], ctx_size - 1)
    kv_out[...] = kv_back[...]
    settle(sum_in, recv_sems.at[5], ctx_size - 1)
    basis_out[...] = sum_in[...]

    settle(raw_in, send_sems.at[0], ctx_size - 1)
    settle(part_in, send_sems.at[1], ctx_size - 1)
    settle(mq_back, send_sems.at[2], ctx_size - 1)
    settle(kv_back, send_sems.at[3], ctx_size - 1)
    settle(half_buf, send_sems.at[4], tp_size - 1)
    settle(sum_in, send_sems.at[5], ctx_size - 1)


def unpack_kernel(
    dims,
    mq_ref,
    kv_ref,
    proj_ref,
    basis_ref,
    mixed_out,
    query_out,
    key_out,
    value_out,
    proj_out,
    basis_out,
):
    ctx_size, chans, folds, share = dims
    feat = ctx_size * share
    group = max(1, 16 // chans)
    for source, index, target in (
        (mq_ref, 0, mixed_out),
        (mq_ref, 1, query_out),
        (kv_ref, 0, key_out),
        (kv_ref, 1, value_out),
    ):
        for first in range(0, ctx_size, group):
            pieces = [source[first + other, index].astype(F32) for other in range(group)]
            for fold in range(folds):
                target[
                    first * chans : (first + group) * chans, fold * LANES : (fold + 1) * LANES
                ] = jnp.concatenate(
                    [piece[fold * chans : (fold + 1) * chans] for piece in pieces], axis=0
                ).astype(BF16)
    proj = jnp.concatenate([proj_ref[source] for source in range(ctx_size)], axis=0)
    proj_out[...] = jnp.transpose(proj)[:feat]
    basis = jnp.concatenate([basis_ref[source] for source in range(ctx_size)], axis=0)
    basis_out[...] = jnp.transpose(basis)[: basis_out.shape[0]]


def on_device(
    tables,
    query_in,
    key_in,
    value_in,
    short_kernel,
    basis_weight,
    basis_bias,
    filter_proj,
    decay_rate,
    skip_gain,
    grad_out,
):
    ctx_size = lax.axis_size("ctx")
    tp_size = lax.axis_size("tp")
    chan_local, num_tok = query_in.shape
    seq_total = num_tok * ctx_size
    chans = chan_local // ctx_size
    taps = short_kernel.shape[2]
    feat, emb = basis_weight.shape
    folds = num_tok // LANES
    slab = folds * chans
    blocks = seq_total // LANES
    rows = blocks * chans

    share = feat // ctx_size
    raw_slabs = (ctx_size, 4, slab, LANES)
    slabs = (ctx_size, 2, slab, LANES)
    dims = (ctx_size, tp_size, chans, seq_total, taps, feat, emb, chan_local * tp_size)
    vmem = pl.BlockSpec(memory_space=pltpu.VMEM)
    anywhere = pl.BlockSpec(memory_space=pl.ANY)
    landed = pl.pallas_call(
        functools.partial(mixer_kernel, dims),
        out_shape=(
            jax.ShapeDtypeStruct(slabs, BF16),
            jax.ShapeDtypeStruct(slabs, BF16),
            jax.ShapeDtypeStruct((ctx_size, chans, LANES), F32),
            jax.ShapeDtypeStruct((ctx_size, share, LANES), F32),
        ),
        in_specs=[vmem] * 10 + [anywhere] * len(tables),
        out_specs=(vmem, vmem, vmem, vmem),
        scratch_shapes=[pltpu.VMEM(table.shape, table.dtype) for table in tables]
        + [
            pltpu.VMEM(raw_slabs, BF16),
            pltpu.VMEM((LANES, chan_local), F32),
            pltpu.VMEM((chan_local, LANES), F32),
            pltpu.VMEM((BAND, LANES), F32),
            pltpu.VMEM(raw_slabs, BF16),
            pltpu.VMEM(slabs, BF16),
            pltpu.VMEM(slabs, BF16),
            pltpu.VMEM(slabs, BF16),
            pltpu.VMEM(slabs, BF16),
            pltpu.VMEM((2 * feat, seq_total), BF16),
            pltpu.VMEM((feat, seq_total), F32),
            pltpu.VMEM((rows, LANES), F32),
            pltpu.VMEM((rows, LANES), F32),
            pltpu.VMEM((ctx_size, chans + share, LANES), F32),
            pltpu.VMEM((ctx_size, chans + share, LANES), F32),
            pltpu.VMEM((tp_size, share, LANES), F32),
            pltpu.VMEM((share, LANES), F32),
            pltpu.VMEM((ctx_size, share, LANES), F32),
            pltpu.SemaphoreType.DMA((6,)),
            pltpu.SemaphoreType.DMA((6,)),
            pltpu.SemaphoreType.DMA((len(tables),)),
        ],
        compiler_params=pltpu.CompilerParams(
            collective_id=0, has_side_effects=True, vmem_limit_bytes=56 * 1024 * 1024
        ),
    )(
        query_in,
        key_in,
        value_in,
        grad_out,
        short_kernel.transpose(0, 2, 1),
        basis_weight.T,
        basis_bias[None, :],
        filter_proj.T,
        decay_rate[None, :],
        skip_gain[None, :],
        *tables,
    )
    block = jax.ShapeDtypeStruct((chan_local, num_tok), BF16)
    mixed, grad_query, grad_key, grad_value, proj_turned, basis_turned = pl.pallas_call(
        functools.partial(unpack_kernel, (ctx_size, chans, folds, share)),
        out_shape=(
            block,
            block,
            block,
            block,
            jax.ShapeDtypeStruct((feat, chan_local), F32),
            jax.ShapeDtypeStruct((emb, feat), F32),
        ),
        in_specs=[vmem] * 4,
        out_specs=(vmem,) * 6,
    )(*landed)
    return (mixed, grad_query, grad_key, grad_value, proj_turned.T, basis_turned.T)


def solution(mesh):
    ctx_size = mesh.shape["ctx"]

    def whole(*args):
        chans = args[0].shape[0] // mesh.shape["tp"] // ctx_size
        num_freq = (args[4].shape[1] - 1) // 2
        tables = constant_tables(args[0].shape[1], chans, num_freq)
        tables = tuple(jnp.asarray(table) for table in tables)
        return jax.shard_map(
            on_device,
            mesh=mesh,
            in_specs=(
                (P(),) * len(tables),
                P("tp", "ctx"),
                P("tp", "ctx"),
                P("tp", "ctx"),
                P(None, "tp", None),
                P(),
                P(),
                P("tp", None),
                P("tp"),
                P("tp"),
                P("tp", "ctx"),
            ),
            out_specs=(
                P("tp", "ctx"),
                P("tp", "ctx"),
                P("tp", "ctx"),
                P("tp", "ctx"),
                P("tp", None),
                P(),
            ),
            check_vma=False,
        )(tables, *args)

    return whole
```
